1024 devices in a mesh: dp: 32 (over x, z_hi, core), table: 32 (over z_lo, y).
Axes of the slice: x: 4, y: 4, z: 32 (z_hi: 4, z_lo: 8; z = z_hi * 8 + z_lo), core: 2. Of those that a mesh axis runs over, the one named last changes fastest.
Arguments:
- sparse_index: int32 [131072, 32], P(('dp', 'table')), may hold values from 0 to 34815, as said below
- frequent_rows: float32 [2048, 128], replicated, may hold values from -3 to 3
- frequent_history: float32 [2048, 128], replicated, may hold values from 0.05 to 2
- owned_rows: float32 [32768, 128], P('table'), may hold values from -3 to 3
- owned_history: float32 [32768, 128], P('table'), may hold values from 0.05 to 2
- pooled_grad: bfloat16 [131072, 1024], P(('dp', 'table')), may hold values from -0.119628906 to 0.119628906
Outputs:
- pooled: bfloat16 [131072, 1024], P(('dp', 'table'))
- updated_frequent: float32 [2048, 128], replicated
- updated_owned: float32 [32768, 128], P('table')
- history_frequent: float32 [2048, 128], replicated
- history_owned: float32 [32768, 128], P('table')
The draws below stay inside these ranges and needn't reach their ends.
Inputs may be any that keep to these rules, and one draw needn't show every extreme that they name: `sparse_index`: infrequent row r (hybrid row 2048 + r) belongs to owner r // 1024. Among the lookups of one device (its 128 samples), at most 32 name infrequent rows of one owner; in every data group one owner receives exactly 32 from every device of the group.
All inputs are finite; a program needn't handle non-finite values.
Results may differ from the reference program's by a relative error of at most 0.013.
Values may be sent and summed in bfloat16 or wider, within the bound.
No kernel may reach another device: no remote copies, remote signals or barrier semaphores. Data moves between devices by JAX's collectives and lax.ppermute only.
A program may use at most 32 MiB of HBM per device.

```python
import math
import jax
import jax.numpy as jnp
from jax import lax

E = 128
F = 8
H = 4
B = 128
NF = 2048
RO = 1024
CAP = 32
NI = 32768
SAMPLES = 131072
N_DP = 32


def draw_sparse_index(key, part):
    key = jax.random.fold_in(key, 11)
    subkeys = jax.random.split(key, 5)
    lookups = B * F * H
    devices = SAMPLES // B
    owners = NI // RO
    fullest = jax.random.randint(subkeys[0], (devices // owners,), 0, owners)
    counts = jax.random.randint(subkeys[1], (devices, owners), CAP // 3, CAP + 1)
    forced = jnp.repeat(fullest, owners)
    counts = jnp.where(jnp.arange(owners)[None, :] == forced[:, None], CAP, counts)
    bounds = jnp.cumsum(counts, axis=1)
    ordering = jax.vmap(lambda subkey: jax.random.permutation(subkey, lookups))(jax.random.split(subkeys[2], devices))
    owner_of = jnp.sum((ordering[:, :, None] >= bounds[:, None, :]).astype(jnp.int32), axis=2)
    remote = ordering < bounds[:, -1:]
    within = jax.random.randint(subkeys[3], (devices, lookups), 0, RO)
    frequent = jax.random.randint(subkeys[4], (devices, lookups), 0, NF)
    chosen = jnp.where(remote, NF + jnp.minimum(owner_of, owners - 1) * RO + within, frequent)
    return chosen.reshape(SAMPLES, F * H).astype(jnp.int32)


def shard_levels(rng, dims, shards, low, largest):
    level, own = 1.0, jax.random.fold_in(rng, 6)
    for dim, shards_of in shards:
        heights = jnp.exp(jax.random.uniform(jax.random.fold_in(own, dim), (shards_of,), jnp.float32, low / len(shards), largest / len(shards)))
        level = level * jnp.repeat(heights, dims[dim] // shards_of).reshape([-1 if axis == dim else 1 for axis in range(len(dims))])
    return level


def normal_values(stream_key, dims, scale, most, cuts=(), dtype=jnp.bfloat16):
    array = scale * jax.random.normal(stream_key, dims, jnp.float32)
    if cuts:
        array = array * shard_levels(stream_key, dims, cuts, -0.22, 0.18)
    return jnp.clip(array, -most, most).astype(dtype)


def setup_inputs(seed: int = 0) -> dict:
    arg_keys = jax.random.split(jax.random.key(seed), 7)
    return {
        "sparse_index": draw_sparse_index(jax.random.fold_in(arg_keys[6], 71), 0),
        "frequent_rows": normal_values(arg_keys[1], (NF, E), 0.5, 3.0, (), jnp.float32),
        "frequent_history": jnp.clip(jnp.exp(jax.random.uniform(arg_keys[2], (NF, E), jnp.float32, math.log(0.05), math.log(2.0))), 0.05, 2.0),
        "owned_rows": normal_values(arg_keys[3], (NI, E), 0.5, 3.0, ((0, 32),), jnp.float32),
        "owned_history": jnp.clip(jnp.exp(math.log(2.0) - 3.6888794 * jax.random.uniform(arg_keys[4], (NI, E), jnp.float32) ** shard_levels(arg_keys[4], (NI, E), ((0, 32),), -0.2, 0.2)), 0.05, 2.0),
        "pooled_grad": normal_values(arg_keys[5], (SAMPLES, F * E), 0.02, 0.119628906, ((0, 1024),)),
    }


def adagrad(weights, history, gradient):
    updated = history + gradient * gradient
    return (weights - 0.5 * gradient / jnp.sqrt(updated + 1e-08), updated)

def reference(sparse_index, frequent_rows, frequent_history, owned_rows, owned_history, pooled_grad):
    frequent_count = frequent_rows.shape[0]
    hybrid = jnp.concatenate([frequent_rows, owned_rows], 0).astype(jnp.bfloat16)
    index_groups = sparse_index.astype(jnp.int32).reshape(N_DP, -1, F * H)
    grad_groups = pooled_grad.reshape(N_DP, -1, F, E)

    def advance(summed, pieces):
        positions, grads = pieces
        fetched = hybrid[positions].astype(jnp.float32)
        pooled_block = lax.optimization_barrier(jnp.sum(fetched.reshape(-1, F, H, E), axis=2)).reshape(-1, F * E).astype(jnp.bfloat16)
        spread = jnp.broadcast_to(grads[:, :, None, :], (grads.shape[0], F, H, E)).reshape(-1, E).astype(jnp.float32)
        summed = summed.at[positions.reshape(-1)].add(spread)
        return (summed, pooled_block)
    start = jnp.zeros(hybrid.shape, jnp.float32)
    gradient, pooled_blocks = lax.scan(advance, start, (index_groups, grad_groups))
    pooled = pooled_blocks.reshape(-1, F * E)
    updated_frequent, history_frequent = adagrad(frequent_rows, frequent_history, gradient[:frequent_count])
    updated_owned, history_owned = adagrad(owned_rows, owned_history, gradient[frequent_count:])
    return (pooled, updated_frequent, updated_owned, history_frequent, history_owned)
```

```python
import functools
import jax
import jax.numpy as jnp
from jax import lax
from jax.experimental import pallas as pl
from jax.experimental.pallas import tpu as pltpu
from jax.sharding import Mesh, PartitionSpec as P

E = 128
F = 8
H = 4
B = 128
NF = 2048
RO = 1024
CAP = 32
OWNERS = 32
TAIL = 16
BLOCK = 256
MSG = CAP + TAIL
BF = jnp.bfloat16
F32 = jnp.float32
NT = (((1,), (1,)), ((), ()))
TN = (((0,), (0,)), ((), ()))


def call(kernel, outs, *args, flops=0, aliases=None):
    moved = sum(a.size * a.dtype.itemsize for a in args)
    moved += sum(o.size * o.dtype.itemsize for o in outs)
    return pl.pallas_call(
        kernel,
        out_shape=outs,
        in_specs=[pl.BlockSpec(memory_space=pltpu.VMEM)] * len(args),
        out_specs=[pl.BlockSpec(memory_space=pltpu.VMEM)] * len(outs),
        input_output_aliases=aliases or {},
        compiler_params=pltpu.CompilerParams(vmem_limit_bytes=40 * 1024 * 1024),
        cost_estimate=pl.CostEstimate(flops=flops, bytes_accessed=moved, transcendentals=0),
    )(*args)


def sds(shape, dtype):
    return jax.ShapeDtypeStruct(shape, dtype)


def onehot(positions, base):
    near = (positions - base).astype(F32).astype(BF)
    rows = lax.broadcasted_iota(jnp.int32, (BLOCK, positions.shape[1]), 0).astype(F32).astype(BF)
    total = None
    for i in range(positions.shape[0]):
        hit = jnp.where(rows == near[i : i + 1], jnp.ones((), BF), jnp.zeros((), BF))
        total = hit if total is None else total + hit
    return total


def counts(positions, base):
    return jnp.concatenate([onehot(positions[f * H : (f + 1) * H], base) for f in range(F)], axis=1)


def stack_tables(grad):
    return jnp.concatenate([grad[:, f * E : (f + 1) * E] for f in range(F)], axis=0)


def frequent_kernel(index_ref, grad_ref, part_ref):
    index = index_ref[...].T
    grad = stack_tables(grad_ref[...])
    for base in range(0, NF, BLOCK):
        part = jnp.dot(counts(index, base), grad, preferred_element_type=F32)
        part_ref[base : base + BLOCK, :] = part.astype(BF)


def slots_kernel(index_ref, grad_ref, msg_ref, req_ref, slot_ref):
    index = index_ref[...].T
    remote = index >= NF
    offset = index - NF
    owner = jnp.where(remote, offset // RO, -1)
    wanted = offset % RO + 1
    high = (wanted // 32).astype(F32)
    low = (wanted % 32).astype(F32)
    owners = lax.broadcasted_iota(jnp.int32, (OWNERS, B), 0)
    masks = [
        jnp.where(owners == owner[i : i + 1], 1.0, 0.0).astype(F32) for i in range(F * H)
    ]
    mask = jnp.concatenate(masks, axis=0).astype(BF)
    row = lax.broadcasted_iota(jnp.int32, (B, 2 * B), 0)
    col = lax.broadcasted_iota(jnp.int32, (B, 2 * B), 1)
    ones = jnp.where((col >= B) | (row < col), 1.0, 0.0).astype(BF)
    earlier = jnp.dot(mask, ones, preferred_element_type=F32)
    run = jnp.zeros((OWNERS, B), F32)
    ranks = []
    for i in range(F * H):
        before = earlier[i * OWNERS : (i + 1) * OWNERS]
        ranks.append(jnp.sum(masks[i] * (before[:, :B] + run), axis=0, keepdims=True))
        run = run + before[:, B:]
    rank = jnp.concatenate(ranks, axis=0)
    slot = jnp.where(remote, owner * CAP + rank.astype(jnp.int32), -1)
    slot_ref[...] = slot
    places = lax.broadcasted_iota(jnp.int32, (B, B), 0).astype(F32)
    what, where = [], []
    for i in range(F * H):
        what.append(
            jnp.concatenate([masks[i] * high[i : i + 1], masks[i] * low[i : i + 1]], axis=0)
        )
        where.append(jnp.where(places == rank[i : i + 1], 1.0, 0.0))
    what = jnp.concatenate(what, axis=1).astype(BF)
    where = jnp.concatenate(where, axis=1).astype(BF)
    req_ref[...] = lax.dot_general(what, where, NT, preferred_element_type=F32)
    grad = stack_tables(grad_ref[...])
    for base in range(0, OWNERS * CAP, BLOCK):
        block = jnp.dot(counts(slot, base), grad, preferred_element_type=F32)
        first = base // CAP
        last = (base + BLOCK) // CAP
        msg_ref[first:last, :CAP, :] = block.astype(BF).reshape(BLOCK // CAP, CAP, E)


def message_kernel(msg_in, req_ref, got_ref, msg_ref):
    del msg_in
    part = jnp.sum(got_ref[...].astype(F32), axis=0)
    parts = part.reshape(4, 8, 8, E)
    line = lax.broadcasted_iota(jnp.int32, (8, E), 0)
    for z in range(8):
        for y in range(4):
            t = z * 4 + y
            high = jnp.where(line == 0, req_ref[t : t + 1, :], 0.0)
            asked = jnp.where(line == 1, req_ref[OWNERS + t : OWNERS + t + 1, :], high)
            msg_ref[t, CAP:, :] = jnp.concatenate([parts[y, z], asked], axis=0).astype(BF)


def owner_kernel(got_ref, rows_ref, part_ref, served_ref, freq_ref):
    tail = got_ref[:, CAP:, :].astype(F32)
    freq_ref[...] = jnp.sum(tail[:, :8, :], axis=0)
    high = jnp.concatenate([tail[t, 8:9, :] for t in range(OWNERS)], axis=0)
    low = jnp.concatenate([tail[t, 9:10, :] for t in range(OWNERS)], axis=0)
    source = lax.broadcasted_iota(jnp.int32, (OWNERS, E), 0) % 4

    def placed(x):
        y = x
        for k in range(1, 4):
            y = jnp.where(source == k, pltpu.roll(x, CAP * k, 1), y)
        return y

    group = lax.broadcasted_iota(jnp.int32, (8, OWNERS), 0)
    member = lax.broadcasted_iota(jnp.int32, (8, OWNERS), 1) // 4
    fold = jnp.where(group == member, 1.0, 0.0).astype(BF)
    high = jnp.dot(fold, placed(high).astype(BF), preferred_element_type=F32)
    low = jnp.dot(fold, placed(low).astype(BF), preferred_element_type=F32)
    wanted = (high * 32.0 + low).astype(jnp.int32) - 1
    grads = got_ref[:, :CAP, :].reshape(OWNERS * CAP, E)
    served = jnp.zeros((OWNERS * CAP, E), F32)
    for base in range(0, RO, BLOCK):
        hits = jnp.concatenate([onehot(wanted[g : g + 1], base) for g in range(8)], axis=1)
        part = jnp.dot(hits, grads, preferred_element_type=F32)
        part_ref[base : base + BLOCK, :] = part.astype(BF)
        rows = rows_ref[base : base + BLOCK, :].astype(BF)
        served = served + lax.dot_general(hits, rows, TN, preferred_element_type=F32)
    served_ref[...] = served.astype(BF).reshape(OWNERS, CAP, E)


def slice_kernel(got_ref, freq_ref, out_ref):
    part = jnp.sum(got_ref[...].astype(F32), axis=0)
    freq = jnp.concatenate([freq_ref[...], jnp.zeros((8, E), F32)], axis=0)
    both = jnp.concatenate([part, freq], axis=0).astype(BF)
    for i in range(4):
        out_ref[i] = both


def total_kernel(got_ref, owned_ref, freq_ref):
    total = jnp.sum(got_ref[...].astype(F32), axis=0)
    owned = total[: RO // 8].astype(BF)
    for i in range(8):
        owned_ref[i] = owned
        freq_ref[i] = total[RO // 8 : RO // 8 + 8]


def spread_kernel(got_ref, out_ref):
    rows = got_ref[...].reshape(64, E).astype(BF)
    for i in range(32):
        out_ref[i] = rows


def pool_frequent_kernel(index_ref, rows_ref, out_ref):
    index = index_ref[...].T
    total = jnp.zeros((F * B, E), F32)
    for base in range(0, NF, BLOCK):
        rows = rows_ref[base : base + BLOCK, :].astype(BF)
        total = total + lax.dot_general(
            counts(index, base), rows, TN, preferred_element_type=F32
        )
    out_ref[...] = total


def pool_kernel(slot_ref, rows_ref, part_ref, out_ref):
    slot = slot_ref[...]
    total = part_ref[...]
    for base in range(0, OWNERS * CAP, BLOCK):
        rows = rows_ref[base : base + BLOCK, :]
        total = total + lax.dot_general(
            counts(slot, base), rows, TN, preferred_element_type=F32
        )
    for f in range(F):
        out_ref[:, f * E : (f + 1) * E] = total[f * B : (f + 1) * B].astype(BF)


def adagrad_kernel(rows_ref, history_ref, grad_ref, updated_ref, new_ref):
    grad = grad_ref[...].astype(F32)
    new = history_ref[...] + grad * grad
    new_ref[...] = new
    updated_ref[...] = rows_ref[...] - 0.5 * grad / jnp.sqrt(new + 1e-08)


def adagrad(rows, history, grad):
    shape = sds(rows.shape, F32)
    return call(adagrad_kernel, [shape, shape], rows, history, grad)


def swap(x, axes):
    return lax.all_to_all(x, axes, split_axis=0, concat_axis=0, tiled=True)


def body(index, frequent_rows, frequent_history, owned_rows, owned_history, grad):
    near, table = ("x", "core"), ("z_lo", "y")
    flat = F * B
    part = call(
        frequent_kernel, [sds((NF, E), BF)], index, grad, flops=2 * NF * flat * E
    )[0]
    part = swap(part.reshape(8, NF // 8, E), near)
    msg, req, slot = call(
        slots_kernel,
        [
            sds((OWNERS, MSG, E), BF),
            sds((2 * OWNERS, E), F32),
            sds((F * H, B), jnp.int32),
        ],
        index,
        grad,
        flops=2 * RO * flat * E,
    )
    msg = call(message_kernel, [sds((OWNERS, MSG, E), BF)], msg, req, part, aliases={0: 0})[0]
    got = swap(msg, table)
    owned, served, freq = call(
        owner_kernel,
        [sds((RO, E), BF), sds((OWNERS, CAP, E), BF), sds((8, E), F32)],
        got,
        owned_rows,
        flops=4 * RO * RO * E,
    )
    owned = swap(owned.reshape(8, RO // 8, E), near)
    both = call(slice_kernel, [sds((4, RO // 8 + 16, E), BF)], owned, freq)[0]
    both = swap(both, "z_hi")
    owned, freq = call(total_kernel, [sds((8, RO // 8, E), BF), sds((8, 8, E), F32)], both)
    freq = swap(freq, "z_lo")
    owned = swap(owned, near)
    freq = call(spread_kernel, [sds((32, 64, E), BF)], freq)[0]
    freq = swap(freq, ("x", "core", "y"))
    returned = swap(served, table).reshape(OWNERS * CAP, E)
    pooled = call(
        pool_frequent_kernel, [sds((flat, E), F32)], index, frequent_rows, flops=2 * NF * flat * E
    )[0]
    pooled = call(
        pool_kernel, [sds((B, F * E), BF)], slot, returned, pooled, flops=2 * RO * flat * E
    )[0]
    updated_owned, history_owned = adagrad(owned_rows, owned_history, owned.reshape(RO, E))
    updated_frequent, history_frequent = adagrad(
        frequent_rows, frequent_history, freq.reshape(NF, E)
    )
    return (pooled, updated_frequent, updated_owned, history_frequent, history_owned)


def solution(mesh):
    fine = Mesh(mesh.devices.reshape(4, 4, 2, 8, 4), ("x", "z_hi", "core", "z_lo", "y"))
    samples, table = ("x", "z_hi", "core", "z_lo", "y"), ("z_lo", "y")
    in_specs = (P(samples, None), P(), P(), P(table, None), P(table, None), P(samples, None))
    out_specs = (P(samples, None), P(), P(table, None), P(), P(table, None))
    return jax.shard_map(body, mesh=fine, in_specs=in_specs, out_specs=out_specs, check_vma=False)
```

```python
import functools
import jax
import jax.numpy as jnp
from jax import lax
from jax.experimental import pallas as pl
from jax.experimental.pallas import tpu as pltpu
from jax.sharding import Mesh, PartitionSpec as P

E = 128
F = 8
H = 4
B = 128
NF = 2048
RO = 1024
CAP = 32
OWNERS = 32
TAIL = 16
BLOCK = 256
MSG = CAP + TAIL
BF = jnp.bfloat16
F32 = jnp.float32
NT = (((1,), (1,)), ((), ()))
TN = (((0,), (0,)), ((), ()))


def call(kernel, outs, *args, flops=0, aliases=None):
    moved = sum(a.size * a.dtype.itemsize for a in args)
    moved += sum(o.size * o.dtype.itemsize for o in outs)
    return pl.pallas_call(
        kernel,
        out_shape=outs,
        in_specs=[pl.BlockSpec(memory_space=pltpu.VMEM)] * len(args),
        out_specs=[pl.BlockSpec(memory_space=pltpu.VMEM)] * len(outs),
        input_output_aliases=aliases or {},
        compiler_params=pltpu.CompilerParams(vmem_limit_bytes=40 * 1024 * 1024),
        cost_estimate=pl.CostEstimate(flops=flops, bytes_accessed=moved, transcendentals=0),
    )(*args)


def sds(shape, dtype):
    return jax.ShapeDtypeStruct(shape, dtype)


def onehot(positions, base):
    near = (positions - base).astype(F32).astype(BF)
    rows = lax.broadcasted_iota(jnp.int32, (BLOCK, positions.shape[1]), 0).astype(F32).astype(BF)
    total = None
    for i in range(positions.shape[0]):
        hit = jnp.where(rows == near[i : i + 1], jnp.ones((), BF), jnp.zeros((), BF))
        total = hit if total is None else total + hit
    return total


def counts(positions, base):
    return jnp.concatenate([onehot(positions[f * H : (f + 1) * H], base) for f in range(F)], axis=1)


def stack_tables(grad):
    return jnp.concatenate([grad[:, f * E : (f + 1) * E] for f in range(F)], axis=0)


def frequent_kernel(index_ref, grad_ref, part_ref):
    index = index_ref[...].T
    grad = stack_tables(grad_ref[...])
    for base in range(0, NF, BLOCK):
        part = jnp.dot(counts(index, base), grad, preferred_element_type=F32)
        part_ref[base : base + BLOCK, :] = part.astype(BF)


def slots_kernel(index_ref, grad_ref, msg_ref, req_ref, slot_ref):
    index = index_ref[...].T
    remote = index >= NF
    offset = index - NF
    owner = jnp.where(remote, offset // RO, -1)
    wanted = offset % RO + 1
    high = (wanted // 32).astype(F32)
    low = (wanted % 32).astype(F32)
    owners = lax.broadcasted_iota(jnp.int32, (OWNERS, B), 0)
    masks = [
        jnp.where(owners == owner[i : i + 1], 1.0, 0.0).astype(F32) for i in range(F * H)
    ]
    mask = jnp.concatenate(masks, axis=0).astype(BF)
    row = lax.broadcasted_iota(jnp.int32, (B, 2 * B), 0)
    col = lax.broadcasted_iota(jnp.int32, (B, 2 * B), 1)
    ones = jnp.where((col >= B) | (row < col), 1.0, 0.0).astype(BF)
    earlier = jnp.dot(mask, ones, preferred_element_type=F32)
    run = jnp.zeros((OWNERS, B), F32)
    ranks = []
    for i in range(F * H):
        before = earlier[i * OWNERS : (i + 1) * OWNERS]
        ranks.append(jnp.sum(masks[i] * (before[:, :B] + run), axis=0, keepdims=True))
        run = run + before[:, B:]
    rank = jnp.concatenate(ranks, axis=0)
    slot = jnp.where(remote, owner * CAP + rank.astype(jnp.int32), -1)
    slot_ref[...] = slot
    places = lax.broadcasted_iota(jnp.int32, (B, B), 0).astype(F32)
    what, where = [], []
    for i in range(F * H):
        what.append(
            jnp.concatenate([masks[i] * high[i : i + 1], masks[i] * low[i : i + 1]], axis=0)
        )
        where.append(jnp.where(places == rank[i : i + 1], 1.0, 0.0))
    what = jnp.concatenate(what, axis=1).astype(BF)
    where = jnp.concatenate(where, axis=1).astype(BF)
    req_ref[...] = lax.dot_general(what, where, NT, preferred_element_type=F32)
    grad = stack_tables(grad_ref[...])
    for base in range(0, OWNERS * CAP, BLOCK):
        block = jnp.dot(counts(slot, base), grad, preferred_element_type=F32)
        first = base // CAP
        last = (base + BLOCK) // CAP
        msg_ref[first:last, :CAP, :] = block.astype(BF).reshape(BLOCK // CAP, CAP, E)


def message_kernel(msg_in, req_ref, got_ref, msg_ref):
    del msg_in
    part = jnp.sum(got_ref[...].astype(F32), axis=0)
    parts = part.reshape(4, 8, 8, E)
    line = lax.broadcasted_iota(jnp.int32, (8, E), 0)
    for z in range(8):
        for y in range(4):
            t = z * 4 + y
            high = jnp.where(line == 0, req_ref[t : t + 1, :], 0.0)
            asked = jnp.where(line == 1, req_ref[OWNERS + t : OWNERS + t + 1, :], high)
            msg_ref[t, CAP:, :] = jnp.concatenate([parts[y, z], asked], axis=0).astype(BF)


def owner_kernel(got_ref, rows_ref, part_ref, served_ref, freq_ref):
    tail = got_ref[:, CAP:, :].astype(F32)
    freq_ref[...] = jnp.sum(tail[:, :8, :], axis=0)
    high = jnp.concatenate([tail[t, 8:9, :] for t in range(OWNERS)], axis=0)
    low = jnp.concatenate([tail[t, 9:10, :] for t in range(OWNERS)], axis=0)
    source = lax.broadcasted_iota(jnp.int32, (OWNERS, E), 0) % 4

    def placed(x):
        y = x
        for k in range(1, 4):
            y = jnp.where(source == k, pltpu.roll(x, CAP * k, 1), y)
        return y

    group = lax.broadcasted_iota(jnp.int32, (8, OWNERS), 0)
    member = lax.broadcasted_iota(jnp.int32, (8, OWNERS), 1) // 4
    fold = jnp.where(group == member, 1.0, 0.0).astype(BF)
    high = jnp.dot(fold, placed(high).astype(BF), preferred_element_type=F32)
    low = jnp.dot(fold, placed(low).astype(BF), preferred_element_type=F32)
    wanted = (high * 32.0 + low).astype(jnp.int32) - 1
    grads = got_ref[:, :CAP, :].reshape(OWNERS * CAP, E)
    served = jnp.zeros((OWNERS * CAP, E), F32)
    for base in range(0, RO, BLOCK):
        hits = jnp.concatenate([onehot(wanted[g : g + 1], base) for g in range(8)], axis=1)
        part = jnp.dot(hits, grads, preferred_element_type=F32)
        part_ref[base : base + BLOCK, :] = part.astype(BF)
        rows = rows_ref[base : base + BLOCK, :].astype(BF)
        served = served + lax.dot_general(hits, rows, TN, preferred_element_type=F32)
    served_ref[...] = served.astype(BF).reshape(OWNERS, CAP, E)


def slice_kernel(got_ref, freq_ref, out_ref):
    part = jnp.sum(got_ref[...].astype(F32), axis=0)
    freq = jnp.concatenate([freq_ref[...], jnp.zeros((8, E), F32)], axis=0)
    both = jnp.concatenate([part, freq], axis=0).astype(BF)
    for i in range(4):
        out_ref[i] = both


def total_kernel(got_ref, served_ref, msg_ref, owned_ref):
    total = jnp.sum(got_ref[...].astype(F32), axis=0)
    owned_ref[...] = total[: RO // 8].astype(BF)
    freq = total[RO // 8 : RO // 8 + 8].astype(BF)
    for t in range(OWNERS):
        msg_ref[t] = jnp.concatenate([served_ref[t], freq], axis=0)


def spread_kernel(got_ref, owned_ref, out_ref):
    freq = [got_ref[z * 4 + y].astype(F32)[CAP:] for y in range(4) for z in range(8)]
    rows = jnp.concatenate([jnp.concatenate(freq, axis=0).astype(BF), owned_ref[...]], axis=0)
    for i in range(8):
        out_ref[i] = rows


def pool_frequent_kernel(index_ref, rows_ref, out_ref):
    index = index_ref[...].T
    total = jnp.zeros((F * B, E), F32)
    for base in range(0, NF, BLOCK):
        rows = rows_ref[base : base + BLOCK, :].astype(BF)
        total = total + lax.dot_general(
            counts(index, base), rows, TN, preferred_element_type=F32
        )
    out_ref[...] = total


def pool_kernel(slot_ref, rows_ref, part_ref, out_ref):
    slot = slot_ref[...]
    total = part_ref[...]
    for base in range(0, OWNERS * CAP, BLOCK):
        rows = rows_ref[base // CAP : (base + BLOCK) // CAP, :CAP, :].reshape(BLOCK, E)
        total = total + lax.dot_general(
            counts(slot, base), rows, TN, preferred_element_type=F32
        )
    for f in range(F):
        out_ref[:, f * E : (f + 1) * E] = total[f * B : (f + 1) * B].astype(BF)


def adagrad(rows, history, grad):
    grad = grad.astype(F32)
    new = history + grad * grad
    return rows - 0.5 * grad / jnp.sqrt(new + 1e-08), new


def adagrad_kernel(
    got_ref, rows_ref, history_ref, owned_ref, owned_history_ref,
    updated_ref, new_ref, updated_owned_ref, new_owned_ref,
):
    part = NF // 8
    for i in range(8):
        at = pl.ds(i * part, part)
        updated_ref[at, :], new_ref[at, :] = adagrad(
            rows_ref[at, :], history_ref[at, :], got_ref[i, :part, :]
        )
        at = pl.ds(i * (RO // 8), RO // 8)
        updated_owned_ref[at, :], new_owned_ref[at, :] = adagrad(
            owned_ref[at, :], owned_history_ref[at, :], got_ref[i, part:, :]
        )


def swap(x, axes):
    return lax.all_to_all(x, axes, split_axis=0, concat_axis=0, tiled=True)


def body(index, frequent_rows, frequent_history, owned_rows, owned_history, grad):
    near, table = ("x", "core"), ("z_lo", "y")
    flat = F * B
    part = call(
        frequent_kernel, [sds((NF, E), BF)], index, grad, flops=2 * NF * flat * E
    )[0]
    part = swap(part.reshape(8, NF // 8, E), near)
    msg, req, slot = call(
        slots_kernel,
        [
            sds((OWNERS, MSG, E), BF),
            sds((2 * OWNERS, E), F32),
            sds((F * H, B), jnp.int32),
        ],
        index,
        grad,
        flops=2 * RO * flat * E,
    )
    msg = call(message_kernel, [sds((OWNERS, MSG, E), BF)], msg, req, part, aliases={0: 0})[0]
    got = swap(msg, table)
    owned, served, freq = call(
        owner_kernel,
        [sds((RO, E), BF), sds((OWNERS, CAP, E), BF), sds((8, E), F32)],
        got,
        owned_rows,
        flops=4 * RO * RO * E,
    )
    owned = swap(owned.reshape(8, RO // 8, E), near)
    both = call(slice_kernel, [sds((4, RO // 8 + 16, E), BF)], owned, freq)[0]
    both = swap(both, "z_hi")
    msg, owned = call(
        total_kernel, [sds((OWNERS, CAP + 8, E), BF), sds((RO // 8, E), BF)], both, served
    )
    got = swap(msg, table)
    both = call(spread_kernel, [sds((8, (NF + RO) // 8, E), BF)], got, owned)[0]
    both = swap(both, near)
    pooled = call(
        pool_frequent_kernel, [sds((flat, E), F32)], index, frequent_rows, flops=2 * NF * flat * E
    )[0]
    pooled = call(
        pool_kernel, [sds((B, F * E), BF)], slot, got, pooled, flops=2 * RO * flat * E
    )[0]
    updated_frequent, history_frequent, updated_owned, history_owned = call(
        adagrad_kernel,
        [sds((NF, E), F32), sds((NF, E), F32), sds((RO, E), F32), sds((RO, E), F32)],
        both,
        frequent_rows,
        frequent_history,
        owned_rows,
        owned_history,
    )
    return (pooled, updated_frequent, updated_owned, history_frequent, history_owned)


def solution(mesh):
    fine = Mesh(mesh.devices.reshape(4, 4, 2, 8, 4), ("x", "z_hi", "core", "z_lo", "y"))
    samples, table = ("x", "z_hi", "core", "z_lo", "y"), ("z_lo", "y")
    in_specs = (P(samples, None), P(), P(), P(table, None), P(table, None), P(samples, None))
    out_specs = (P(samples, None), P(), P(table, None), P(), P(table, None))
    return jax.shard_map(body, mesh=fine, in_specs=in_specs, out_specs=out_specs, check_vma=False)
```

```python
import functools
import jax
import jax.numpy as jnp
from jax import lax
from jax.experimental import pallas as pl
from jax.experimental.pallas import tpu as pltpu
from jax.sharding import Mesh, PartitionSpec as P

E = 128
F = 8
H = 4
B = 128
NF = 2048
RO = 1024
CAP = 32
OWNERS = 32
TAIL = 16
BLOCK = 256
MSG = CAP + TAIL
BF = jnp.bfloat16
F32 = jnp.float32
NT = (((1,), (1,)), ((), ()))
TN = (((0,), (0,)), ((), ()))


def call(kernel, outs, *args, flops=0, aliases=None):
    moved = sum(a.size * a.dtype.itemsize for a in args)
    moved += sum(o.size * o.dtype.itemsize for o in outs)
    return pl.pallas_call(
        kernel,
        out_shape=outs,
        in_specs=[pl.BlockSpec(memory_space=pltpu.VMEM)] * len(args),
        out_specs=[pl.BlockSpec(memory_space=pltpu.VMEM)] * len(outs),
        input_output_aliases=aliases or {},
        compiler_params=pltpu.CompilerParams(vmem_limit_bytes=40 * 1024 * 1024),
        cost_estimate=pl.CostEstimate(flops=flops, bytes_accessed=moved, transcendentals=0),
    )(*args)


def sds(shape, dtype):
    return jax.ShapeDtypeStruct(shape, dtype)


def onehot(positions, base):
    near = (positions - base).astype(F32).astype(BF)
    rows = lax.broadcasted_iota(jnp.int32, (BLOCK, positions.shape[1]), 0).astype(F32).astype(BF)
    total = None
    for i in range(positions.shape[0]):
        hit = jnp.where(rows == near[i : i + 1], jnp.ones((), BF), jnp.zeros((), BF))
        total = hit if total is None else total + hit
    return total


def counts(positions, base):
    return jnp.concatenate([onehot(positions[f * H : (f + 1) * H], base) for f in range(F)], axis=1)


def stack_tables(grad):
    return jnp.concatenate([grad[:, f * E : (f + 1) * E] for f in range(F)], axis=0)


def frequent_kernel(index_ref, grad_ref, part_ref):
    index = index_ref[...].T
    grad = stack_tables(grad_ref[...])
    for base in range(0, NF, BLOCK):
        part = jnp.dot(counts(index, base), grad, preferred_element_type=F32)
        part_ref[base : base + BLOCK, :] = part.astype(BF)


def slots_kernel(index_ref, grad_ref, msg_ref, req_ref, slot_ref):
    index = index_ref[...].T
    remote = index >= NF
    offset = index - NF
    owner = jnp.where(remote, offset // RO, -1)
    wanted = offset % RO + 1
    high = (wanted // 32).astype(F32)
    low = (wanted % 32).astype(F32)
    owners = lax.broadcasted_iota(jnp.int32, (OWNERS, B), 0)
    masks = [
        jnp.where(owners == owner[i : i + 1], 1.0, 0.0).astype(F32) for i in range(F * H)
    ]
    mask = jnp.concatenate(masks, axis=0).astype(BF)
    row = lax.broadcasted_iota(jnp.int32, (B, 2 * B), 0)
    col = lax.broadcasted_iota(jnp.int32, (B, 2 * B), 1)
    ones = jnp.where((col >= B) | (row < col), 1.0, 0.0).astype(BF)
    earlier = jnp.dot(mask, ones, preferred_element_type=F32)
    run = jnp.zeros((OWNERS, B), F32)
    ranks = []
    for i in range(F * H):
        before = earlier[i * OWNERS : (i + 1) * OWNERS]
        ranks.append(jnp.sum(masks[i] * (before[:, :B] + run), axis=0, keepdims=True))
        run = run + before[:, B:]
    rank = jnp.concatenate(ranks, axis=0)
    slot = jnp.where(remote, owner * CAP + rank.astype(jnp.int32), -1)
    slot_ref[...] = slot
    places = lax.broadcasted_iota(jnp.int32, (B, B), 0).astype(F32)
    what, where = [], []
    for i in range(F * H):
        what.append(
            jnp.concatenate([masks[i] * high[i : i + 1], masks[i] * low[i : i + 1]], axis=0)
        )
        where.append(jnp.where(places == rank[i : i + 1], 1.0, 0.0))
    what = jnp.concatenate(what, axis=1).astype(BF)
    where = jnp.concatenate(where, axis=1).astype(BF)
    req_ref[...] = lax.dot_general(what, where, NT, preferred_element_type=F32)
    grad = stack_tables(grad_ref[...])
    for base in range(0, OWNERS * CAP, BLOCK):
        block = jnp.dot(counts(slot, base), grad, preferred_element_type=F32)
        first = base // CAP
        last = (base + BLOCK) // CAP
        msg_ref[first:last, :CAP, :] = block.astype(BF).reshape(BLOCK // CAP, CAP, E)


def message_kernel(msg_in, req_ref, got_ref, msg_ref):
    del msg_in
    part = jnp.sum(got_ref[...].astype(F32), axis=0)
    parts = part.reshape(4, 8, 8, E)
    line = lax.broadcasted_iota(jnp.int32, (8, E), 0)
    for z in range(8):
        for y in range(4):
            t = z * 4 + y
            high = jnp.where(line == 0, req_ref[t : t + 1, :], 0.0)
            asked = jnp.where(line == 1, req_ref[OWNERS + t : OWNERS + t + 1, :], high)
            msg_ref[t, CAP:, :] = jnp.concatenate([parts[y, z], asked], axis=0).astype(BF)


def owner_kernel(got_ref, rows_ref, part_ref, served_ref, freq_ref):
    tail = got_ref[:, CAP:, :].astype(F32)
    freq_ref[...] = jnp.sum(tail[:, :8, :], axis=0)
    high = jnp.concatenate([tail[t, 8:9, :] for t in range(OWNERS)], axis=0)
    low = jnp.concatenate([tail[t, 9:10, :] for t in range(OWNERS)], axis=0)
    source = lax.broadcasted_iota(jnp.int32, (OWNERS, E), 0) % 4

    def placed(x):
        y = x
        for k in range(1, 4):
            y = jnp.where(source == k, pltpu.roll(x, CAP * k, 1), y)
        return y

    group = lax.broadcasted_iota(jnp.int32, (8, OWNERS), 0)
    member = lax.broadcasted_iota(jnp.int32, (8, OWNERS), 1) // 4
    fold = jnp.where(group == member, 1.0, 0.0).astype(BF)
    high = jnp.dot(fold, placed(high).astype(BF), preferred_element_type=F32)
    low = jnp.dot(fold, placed(low).astype(BF), preferred_element_type=F32)
    wanted = (high * 32.0 + low).astype(jnp.int32) - 1
    grads = got_ref[:, :CAP, :].reshape(OWNERS * CAP, E)
    served = jnp.zeros((OWNERS * CAP, E), F32)
    for base in range(0, RO, BLOCK):
        hits = jnp.concatenate([onehot(wanted[g : g + 1], base) for g in range(8)], axis=1)
        part = jnp.dot(hits, grads, preferred_element_type=F32)
        part_ref[base : base + BLOCK, :] = part.astype(BF)
        rows = rows_ref[base : base + BLOCK, :].astype(BF)
        served = served + lax.dot_general(hits, rows, TN, preferred_element_type=F32)
    served_ref[...] = served.astype(BF).reshape(OWNERS, CAP, E)


def slice_kernel(got_ref, freq_ref, out_ref):
    part = jnp.sum(got_ref[...].astype(F32), axis=0)
    freq = jnp.concatenate([freq_ref[...], jnp.zeros((8, E), F32)], axis=0)
    both = jnp.concatenate([part, freq], axis=0).astype(BF)
    out_ref[0] = both


def pair_kernel(a_ref, b_ref, out_ref):
    out_ref[...] = (a_ref[...].astype(F32) + b_ref[...].astype(F32)).astype(BF)


def total_kernel(mine_ref, got_ref, served_ref, msg_ref, owned_ref):
    total = mine_ref[...].astype(F32) + got_ref[...].astype(F32)
    owned_ref[...] = total[: RO // 8].astype(BF)
    freq = total[RO // 8 : RO // 8 + 8].astype(BF)
    for t in range(OWNERS):
        msg_ref[t] = jnp.concatenate([served_ref[t], freq], axis=0)


def spread_kernel(got_ref, owned_ref, out_ref):
    freq = [got_ref[z * 4 + y].astype(F32)[CAP:] for y in range(4) for z in range(8)]
    rows = jnp.concatenate([jnp.concatenate(freq, axis=0).astype(BF), owned_ref[...]], axis=0)
    for i in range(8):
        out_ref[i] = rows


def pool_frequent_kernel(index_ref, rows_ref, out_ref):
    index = index_ref[...].T
    total = jnp.zeros((F * B, E), F32)
    for base in range(0, NF, BLOCK):
        rows = rows_ref[base : base + BLOCK, :].astype(BF)
        total = total + lax.dot_general(
            counts(index, base), rows, TN, preferred_element_type=F32
        )
    out_ref[...] = total


def pool_kernel(slot_ref, rows_ref, part_ref, out_ref):
    slot = slot_ref[...]
    total = part_ref[...]
    for base in range(0, OWNERS * CAP, BLOCK):
        rows = rows_ref[base // CAP : (base + BLOCK) // CAP, :CAP, :].reshape(BLOCK, E)
        total = total + lax.dot_general(
            counts(slot, base), rows, TN, preferred_element_type=F32
        )
    for f in range(F):
        out_ref[:, f * E : (f + 1) * E] = total[f * B : (f + 1) * B].astype(BF)


def adagrad(rows, history, grad):
    grad = grad.astype(F32)
    new = history + grad * grad
    return rows - 0.5 * grad / jnp.sqrt(new + 1e-08), new


def adagrad_kernel(
    got_ref, rows_ref, history_ref, owned_ref, owned_history_ref,
    updated_ref, new_ref, updated_owned_ref, new_owned_ref,
):
    part = NF // 8
    for i in range(8):
        at = pl.ds(i * part, part)
        updated_ref[at, :], new_ref[at, :] = adagrad(
            rows_ref[at, :], history_ref[at, :], got_ref[i, :part, :]
        )
        at = pl.ds(i * (RO // 8), RO // 8)
        updated_owned_ref[at, :], new_owned_ref[at, :] = adagrad(
            owned_ref[at, :], owned_history_ref[at, :], got_ref[i, part:, :]
        )


def swap(x, axes):
    return lax.all_to_all(x, axes, split_axis=0, concat_axis=0, tiled=True)


def body(index, frequent_rows, frequent_history, owned_rows, owned_history, grad):
    near, table = ("x", "core"), ("z_lo", "y")
    flat = F * B
    part = call(
        frequent_kernel, [sds((NF, E), BF)], index, grad, flops=2 * NF * flat * E
    )[0]
    part = swap(part.reshape(8, NF // 8, E), near)
    msg, req, slot = call(
        slots_kernel,
        [
            sds((OWNERS, MSG, E), BF),
            sds((2 * OWNERS, E), F32),
            sds((F * H, B), jnp.int32),
        ],
        index,
        grad,
        flops=2 * RO * flat * E,
    )
    msg = call(message_kernel, [sds((OWNERS, MSG, E), BF)], msg, req, part, aliases={0: 0})[0]
    got = swap(msg, table)
    owned, served, freq = call(
        owner_kernel,
        [sds((RO, E), BF), sds((OWNERS, CAP, E), BF), sds((8, E), F32)],
        got,
        owned_rows,
        flops=4 * RO * RO * E,
    )
    owned = swap(owned.reshape(8, RO // 8, E), near)
    both = call(slice_kernel, [sds((1, RO // 8 + 16, E), BF)], owned, freq)[0]
    both = both[0]
    got = lax.ppermute(both, "z_hi", [(0, 1), (1, 0), (2, 3), (3, 2)])
    both = call(pair_kernel, [sds((RO // 8 + 16, E), BF)], both, got)[0]
    got = lax.ppermute(both, "z_hi", [(1, 2), (2, 1), (3, 0), (0, 3)])
    msg, owned = call(
        total_kernel, [sds((OWNERS, CAP + 8, E), BF), sds((RO // 8, E), BF)], both, got, served
    )
    got = swap(msg, table)
    both = call(spread_kernel, [sds((8, (NF + RO) // 8, E), BF)], got, owned)[0]
    both = swap(both, near)
    pooled = call(
        pool_frequent_kernel, [sds((flat, E), F32)], index, frequent_rows, flops=2 * NF * flat * E
    )[0]
    pooled = call(
        pool_kernel, [sds((B, F * E), BF)], slot, got, pooled, flops=2 * RO * flat * E
    )[0]
    updated_frequent, history_frequent, updated_owned, history_owned = call(
        adagrad_kernel,
        [sds((NF, E), F32), sds((NF, E), F32), sds((RO, E), F32), sds((RO, E), F32)],
        both,
        frequent_rows,
        frequent_history,
        owned_rows,
        owned_history,
    )
    return (pooled, updated_frequent, updated_owned, history_frequent, history_owned)


def solution(mesh):
    fine = Mesh(mesh.devices.reshape(4, 4, 2, 8, 4), ("x", "z_hi", "core", "z_lo", "y"))
    samples, table = ("x", "z_hi", "core", "z_lo", "y"), ("z_lo", "y")
    in_specs = (P(samples, None), P(), P(), P(table, None), P(table, None), P(samples, None))
    out_specs = (P(samples, None), P(), P(table, None), P(), P(table, None))
    return jax.shard_map(body, mesh=fine, in_specs=in_specs, out_specs=out_specs, check_vma=False)
```

```python
import functools
import jax
import jax.numpy as jnp
from jax import lax
from jax.experimental import pallas as pl
from jax.experimental.pallas import tpu as pltpu
from jax.sharding import Mesh, PartitionSpec as P

E = 128
F = 8
H = 4
B = 128
NF = 2048
RO = 1024
CAP = 32
OWNERS = 32
BLOCK = 256
QUARTER = NF // 128
MSG = CAP + QUARTER + 2
PAIR_COST = 10**12
BF = jnp.bfloat16
F32 = jnp.float32
NT = (((1,), (1,)), ((), ()))
TN = (((0,), (0,)), ((), ()))


def call(kernel, outs, *args, flops=0, vmem=40):
    moved = sum(a.size * a.dtype.itemsize for a in args)
    moved += sum(o.size * o.dtype.itemsize for o in outs)
    return pl.pallas_call(
        kernel,
        out_shape=outs,
        in_specs=[
            pl.BlockSpec(memory_space=pltpu.SMEM if len(a.shape) == 1 else pltpu.VMEM)
            for a in args
        ],
        out_specs=[pl.BlockSpec(memory_space=pltpu.VMEM)] * len(outs),
        compiler_params=pltpu.CompilerParams(vmem_limit_bytes=vmem * 1024 * 1024),
        cost_estimate=pl.CostEstimate(flops=flops, bytes_accessed=moved, transcendentals=0),
    )(*args)


def sds(shape, dtype):
    return jax.ShapeDtypeStruct(shape, dtype)


def onehot(positions, base):
    near = (positions - base).astype(F32).astype(BF)
    rows = lax.broadcasted_iota(jnp.int32, (BLOCK, positions.shape[1]), 0).astype(F32).astype(BF)
    total = None
    for i in range(positions.shape[0]):
        hit = jnp.where(rows == near[i : i + 1], jnp.ones((), BF), jnp.zeros((), BF))
        total = hit if total is None else total + hit
    return total


def counts(positions, base):
    return jnp.concatenate([onehot(positions[f * H : (f + 1) * H], base) for f in range(F)], axis=1)


def stack_tables(grad):
    return jnp.concatenate([grad[:, f * E : (f + 1) * E] for f in range(F)], axis=0)


def frequent_kernel(index_ref, grad_ref, part_ref):
    index = index_ref[...].T
    grad = stack_tables(grad_ref[...])
    for base in range(0, NF, BLOCK):
        part = jnp.dot(counts(index, base), grad, preferred_element_type=F32)
        part_ref[base : base + BLOCK, :] = part.astype(BF)


def slots_kernel(index_ref, grad_ref, out_ref, req_ref, slot_ref):
    index = index_ref[...].T
    remote = index >= NF
    offset = index - NF
    owner = jnp.where(remote, offset // RO, -1)
    wanted = offset % RO + 1
    high = (wanted // 32).astype(F32)
    low = (wanted % 32).astype(F32)
    owners = lax.broadcasted_iota(jnp.int32, (OWNERS, B), 0)
    masks = [
        jnp.where(owners == owner[i : i + 1], 1.0, 0.0).astype(F32) for i in range(F * H)
    ]
    mask = jnp.concatenate(masks, axis=0).astype(BF)
    row = lax.broadcasted_iota(jnp.int32, (B, 2 * B), 0)
    col = lax.broadcasted_iota(jnp.int32, (B, 2 * B), 1)
    ones = jnp.where((col >= B) | (row < col), 1.0, 0.0).astype(BF)
    earlier = jnp.dot(mask, ones, preferred_element_type=F32)
    run = jnp.zeros((OWNERS, B), F32)
    ranks = []
    for i in range(F * H):
        before = earlier[i * OWNERS : (i + 1) * OWNERS]
        ranks.append(jnp.sum(masks[i] * (before[:, :B] + run), axis=0, keepdims=True))
        run = run + before[:, B:]
    rank = jnp.concatenate(ranks, axis=0)
    slot = jnp.where(remote, owner * CAP + rank.astype(jnp.int32), -1)
    slot_ref[...] = slot
    places = lax.broadcasted_iota(jnp.int32, (B, B), 0).astype(F32)
    what, where = [], []
    for i in range(F * H):
        what.append(
            jnp.concatenate([masks[i] * high[i : i + 1], masks[i] * low[i : i + 1]], axis=0)
        )
        where.append(jnp.where(places == rank[i : i + 1], 1.0, 0.0))
    what = jnp.concatenate(what, axis=1).astype(BF)
    where = jnp.concatenate(where, axis=1).astype(BF)
    req_ref[...] = lax.dot_general(what, where, NT, preferred_element_type=F32)
    grad = stack_tables(grad_ref[...])
    for base in range(0, OWNERS * CAP, BLOCK):
        block = jnp.dot(counts(slot, base), grad, preferred_element_type=F32)
        first = base // CAP
        last = (base + BLOCK) // CAP
        out_ref[first:last] = block.astype(BF).reshape(BLOCK // CAP, CAP, E)


def message_kernel(slots_ref, req_ref, got_ref, msg_ref):
    part = jnp.sum(got_ref[...].astype(F32), axis=0)
    for t in range(OWNERS):
        row = t % 4 * QUARTER
        high = req_ref[t : t + 1, :]
        low = req_ref[OWNERS + t : OWNERS + t + 1, :]
        tail = jnp.concatenate([part[row : row + QUARTER], high, low], axis=0).astype(BF)
        msg_ref[t] = jnp.concatenate([slots_ref[t], tail], axis=0)


def hits_of(wanted, base):
    return jnp.concatenate([onehot(wanted[g : g + 1], base) for g in range(8)], axis=1)


def owner_kernel(got_ref, part_ref, wanted_ref, freq_ref):
    tails = [got_ref[t].astype(F32)[CAP:] for t in range(OWNERS)]
    quarters = [sum(t[:QUARTER] for t in tails[y::4]) for y in range(4)]
    freq_ref[...] = jnp.concatenate(quarters, axis=0).astype(BF)
    high = jnp.concatenate([t[QUARTER : QUARTER + 1] for t in tails], axis=0)
    low = jnp.concatenate([t[QUARTER + 1 :] for t in tails], axis=0)
    source = lax.broadcasted_iota(jnp.int32, (OWNERS, E), 0) % 4

    def placed(x):
        y = x
        for k in range(1, 4):
            y = jnp.where(source == k, pltpu.roll(x, CAP * k, 1), y)
        return y

    group = lax.broadcasted_iota(jnp.int32, (8, OWNERS), 0)
    member = lax.broadcasted_iota(jnp.int32, (8, OWNERS), 1) // 4
    fold = jnp.where(group == member, 1.0, 0.0).astype(BF)
    high = jnp.dot(fold, placed(high).astype(BF), preferred_element_type=F32)
    low = jnp.dot(fold, placed(low).astype(BF), preferred_element_type=F32)
    wanted = (high * 32.0 + low).astype(jnp.int32) - 1
    wanted_ref[...] = wanted
    grads = jnp.concatenate([got_ref[t][:CAP] for t in range(OWNERS)], axis=0)
    for base in range(0, RO, BLOCK):
        part = jnp.dot(hits_of(wanted, base), grads, preferred_element_type=F32)
        part_ref[base : base + BLOCK, :] = part.astype(BF)


def serve_kernel(wanted_ref, rows_ref, after_ref, out_ref):
    del after_ref
    wanted = wanted_ref[...]
    served = jnp.zeros((OWNERS * CAP, E), F32)
    for base in range(0, RO, BLOCK):
        rows = rows_ref[base : base + BLOCK, :].astype(BF)
        served = served + lax.dot_general(
            hits_of(wanted, base), rows, TN, preferred_element_type=F32
        )
    out_ref[...] = served.astype(BF).reshape(OWNERS, CAP, E)


def slice_kernel(got_ref, freq_ref, out_ref):
    out_ref[: RO // 8, :] = jnp.sum(got_ref[...].astype(F32), axis=0).astype(BF)
    out_ref[RO // 8 :, :] = freq_ref[...]


def pair_kernel(a_ref, b_ref, out_ref):
    out_ref[...] = (a_ref[...].astype(F32) + b_ref[...].astype(F32)).astype(BF)


def total_kernel(mine_ref, got_ref, after_ref, owned_ref, freq_ref):
    del after_ref
    total = (mine_ref[...].astype(F32) + got_ref[...].astype(F32)).astype(BF)
    owned_ref[...] = total[: RO // 8]
    for i in range(4):
        freq_ref[i] = total[RO // 8 :]


def spread_kernel(got_ref, owned_ref, out_ref):
    freq = [
        got_ref[q, y * QUARTER : (y + 1) * QUARTER, :] for y in range(4) for q in range(4)
    ]
    rows = jnp.concatenate(freq + [owned_ref[...]], axis=0)
    for i in range(4):
        out_ref[i] = rows


def pool_frequent_kernel(index_ref, rows_ref, out_ref):
    index = index_ref[...].T
    total = jnp.zeros((F * B, E), F32)
    for base in range(0, NF, BLOCK):
        rows = rows_ref[base : base + BLOCK, :].astype(BF)
        total = total + lax.dot_general(
            counts(index, base), rows, TN, preferred_element_type=F32
        )
    out_ref[...] = total


def pool_kernel(slot_ref, rows_ref, part_ref, out_ref):
    slot = slot_ref[...]
    total = part_ref[...]
    for base in range(0, OWNERS * CAP, BLOCK):
        rows = rows_ref[base : base + BLOCK, :]
        total = total + lax.dot_general(
            counts(slot, base), rows, TN, preferred_element_type=F32
        )
    for f in range(F):
        out_ref[:, f * E : (f + 1) * E] = total[f * B : (f + 1) * B].astype(BF)


def adagrad(rows, history, grad):
    grad = grad.astype(F32)
    new = history + grad * grad
    return rows - 0.5 * grad / jnp.sqrt(new + 1e-08), new


def adagrad_kernel(core_ref, mine_ref, other_ref, rows_ref, history_ref, updated_ref, new_ref):
    core = core_ref[0]
    part = updated_ref.shape[0] // 8
    first = mine_ref.shape[1] - part if part == RO // 8 else 0
    for got_ref, c in ((mine_ref, core), (other_ref, 1 - core)):
        for i in range(4):
            at = pl.ds(pl.multiple_of((2 * i + c) * part, part), part)
            updated_ref[at, :], new_ref[at, :] = adagrad(
                rows_ref[at, :], history_ref[at, :], got_ref[i, first : first + part, :]
            )


def swap(x, axes):
    return lax.all_to_all(x, axes, split_axis=0, concat_axis=0, tiled=True)


def window(z_hi, core, z_lo):
    return (z_hi - (core == 1 and z_lo < 4)) % 4


def z_hi_of(w, core, z_lo):
    return [z for z in range(4) if window(z, core, z_lo) == w][0]


def owner_groups():
    return [
        [
            ((z_hi_of(w, core, z) * 2 + core) * 8 + z) * 4 + y
            for z in range(8)
            for y in range(4)
        ]
        for core in range(2)
        for w in range(4)
    ]


def far_pairs(step):
    pairs = []
    for core in range(2):
        for w in range(4):
            other = w ^ 1 if core == step else (3 - w) % 4
            for z in range(8):
                a, b = z_hi_of(w, core, z), z_hi_of(other, core, z)
                pairs.append(((a * 2 + core) * 8 + z, (b * 2 + core) * 8 + z))
    return pairs


def far(x, step):
    return lax.ppermute(x, ("z_hi", "core", "z_lo"), far_pairs(step))


def to_owners(x):
    return lax.all_to_all(
        x,
        ("z_hi", "core", "z_lo", "y"),
        split_axis=0,
        concat_axis=0,
        tiled=True,
        axis_index_groups=owner_groups(),
    )


def body(index, frequent_rows, frequent_history, owned_rows, owned_history, grad):
    near, plane = ("x", "core"), ("x", "core", "y")
    flat = F * B
    part = call(
        frequent_kernel, [sds((NF, E), BF)], index, grad, flops=2 * NF * flat * E
    )[0]
    part = swap(part.reshape(32, NF // 32, E), plane)
    slots, req, slot = call(
        slots_kernel,
        [
            sds((OWNERS, CAP, E), BF),
            sds((2 * OWNERS, E), F32),
            sds((F * H, B), jnp.int32),
        ],
        index,
        grad,
        flops=2 * RO * flat * E,
    )
    msg = call(message_kernel, [sds((OWNERS, MSG, E), BF)], slots, req, part)[0]
    got = to_owners(msg)
    owned, wanted, freq = call(
        owner_kernel,
        [sds((RO, E), BF), sds((8, E), jnp.int32), sds((NF // 32, E), BF)],
        got,
        flops=2 * RO * RO * E,
    )
    owned = swap(owned.reshape(8, RO // 8, E), near)
    both = call(slice_kernel, [sds((RO // 8 + NF // 32, E), BF)], owned, freq)[0]
    served = call(
        serve_kernel,
        [sds((OWNERS, CAP, E), BF)],
        wanted,
        owned_rows,
        both,
        flops=2 * RO * RO * E,
    )[0]
    returned = to_owners(served)
    got = far(both, 0)
    both = call(pair_kernel, [sds(both.shape, BF)], both, got, flops=PAIR_COST)[0]
    got = far(both, 1)
    got, returned = lax.optimization_barrier((got, returned))
    pooled = call(
        pool_frequent_kernel, [sds((flat, E), F32)], index, frequent_rows, flops=2 * NF * flat * E
    )[0]
    owned, freq = call(
        total_kernel, [sds((RO // 8, E), BF), sds((4, NF // 32, E), BF)], both, got, pooled
    )
    freq = swap(freq, "y")
    both = call(spread_kernel, [sds((4, (NF + RO) // 8, E), BF)], freq, owned)[0]
    mine = swap(both, "x")
    other = lax.ppermute(mine, "core", [(0, 1), (1, 0)])
    pooled = call(
        pool_kernel,
        [sds((B, F * E), BF)],
        slot,
        returned.reshape(OWNERS * CAP, E),
        pooled,
        flops=2 * RO * flat * E,
    )[0]
    core = lax.axis_index("core").reshape(1)
    updated_frequent, history_frequent = call(
        adagrad_kernel, [sds((NF, E), F32)] * 2, core, mine, other, frequent_rows, frequent_history
    )
    updated_owned, history_owned = call(
        adagrad_kernel, [sds((RO, E), F32)] * 2, core, mine, other, owned_rows, owned_history
    )
    return (pooled, updated_frequent, updated_owned, history_frequent, history_owned)


def solution(mesh):
    fine = Mesh(mesh.devices.reshape(4, 4, 2, 8, 4), ("x", "z_hi", "core", "z_lo", "y"))
    samples, table = ("x", "z_hi", "core", "z_lo", "y"), ("z_lo", "y")
    in_specs = (P(samples, None), P(), P(), P(table, None), P(table, None), P(samples, None))
    out_specs = (P(samples, None), P(), P(table, None), P(), P(table, None))
    return jax.shard_map(body, mesh=fine, in_specs=in_specs, out_specs=out_specs, check_vma=False)
```

```python
import functools
import jax
import jax.numpy as jnp
from jax import lax
from jax.experimental import pallas as pl
from jax.experimental.pallas import tpu as pltpu
from jax.sharding import Mesh, PartitionSpec as P

E = 128
F = 8
H = 4
B = 128
NF = 2048
RO = 1024
CAP = 32
OWNERS = 32
BLOCK = 256
PIECE = NF // 256
MSG = CAP + PIECE + 2
PAIR_COST = 10**12
BF = jnp.bfloat16
F32 = jnp.float32
NT = (((1,), (1,)), ((), ()))
TN = (((0,), (0,)), ((), ()))


def call(kernel, outs, *args, flops=0, vmem=40):
    moved = sum(a.size * a.dtype.itemsize for a in args)
    moved += sum(o.size * o.dtype.itemsize for o in outs)
    return pl.pallas_call(
        kernel,
        out_shape=outs,
        in_specs=[
            pl.BlockSpec(memory_space=pltpu.SMEM if len(a.shape) == 1 else pltpu.VMEM)
            for a in args
        ],
        out_specs=[pl.BlockSpec(memory_space=pltpu.VMEM)] * len(outs),
        compiler_params=pltpu.CompilerParams(vmem_limit_bytes=vmem * 1024 * 1024),
        cost_estimate=pl.CostEstimate(flops=flops, bytes_accessed=moved, transcendentals=0),
    )(*args)


def sds(shape, dtype):
    return jax.ShapeDtypeStruct(shape, dtype)


def onehot(positions, base):
    near = (positions - base).astype(F32).astype(BF)
    rows = lax.broadcasted_iota(jnp.int32, (BLOCK, positions.shape[1]), 0).astype(F32).astype(BF)
    total = None
    for i in range(positions.shape[0]):
        hit = jnp.where(rows == near[i : i + 1], jnp.ones((), BF), jnp.zeros((), BF))
        total = hit if total is None else total + hit
    return total


def counts(positions, base):
    return jnp.concatenate([onehot(positions[f * H : (f + 1) * H], base) for f in range(F)], axis=1)


def stack_tables(grad):
    return jnp.concatenate([grad[:, f * E : (f + 1) * E] for f in range(F)], axis=0)


def frequent_kernel(index_hbm, grad_hbm, part_ref, index_ref, grad_ref, sems):
    index_copy = pltpu.make_async_copy(index_hbm, index_ref, sems.at[0])
    grad_copy = pltpu.make_async_copy(grad_hbm, grad_ref, sems.at[1])
    index_copy.start()
    grad_copy.start()
    index_copy.wait()
    index = index_ref[...]
    first = counts(index, 0)
    grad_copy.wait()
    grad = stack_tables(grad_ref[...])
    for base in range(0, NF, BLOCK):
        hits = counts(index, base) if base else first
        part = jnp.dot(hits, grad, preferred_element_type=F32)
        part_ref[base : base + BLOCK, :] = part.astype(BF)


def frequent_part(index, grad):
    return pl.pallas_call(
        frequent_kernel,
        out_shape=sds((NF, E), BF),
        in_specs=[pl.BlockSpec(memory_space=pl.ANY)] * 2,
        out_specs=pl.BlockSpec(memory_space=pltpu.VMEM),
        scratch_shapes=[
            pltpu.VMEM(index.shape, index.dtype),
            pltpu.VMEM(grad.shape, grad.dtype),
            pltpu.SemaphoreType.DMA((2,)),
        ],
        compiler_params=pltpu.CompilerParams(vmem_limit_bytes=60 * 1024 * 1024),
    )(index, grad)


def slots_kernel(index_ref, grad_ref, out_ref, req_ref, slot_ref):
    index = index_ref[...]
    remote = index >= NF
    offset = index - NF
    owner = jnp.where(remote, offset // RO, -1)
    wanted = offset % RO + 1
    high = (wanted // 32).astype(F32)
    low = (wanted % 32).astype(F32)
    owners = lax.broadcasted_iota(jnp.int32, (OWNERS, B), 0)
    masks = [
        jnp.where(owners == owner[i : i + 1], 1.0, 0.0).astype(F32) for i in range(F * H)
    ]
    mask = jnp.concatenate(masks, axis=0).astype(BF)
    row = lax.broadcasted_iota(jnp.int32, (B, 2 * B), 0)
    col = lax.broadcasted_iota(jnp.int32, (B, 2 * B), 1)
    ones = jnp.where((col >= B) | (row < col), 1.0, 0.0).astype(BF)
    earlier = jnp.dot(mask, ones, preferred_element_type=F32)
    run = jnp.zeros((OWNERS, B), F32)
    ranks = []
    for i in range(F * H):
        before = earlier[i * OWNERS : (i + 1) * OWNERS]
        ranks.append(jnp.sum(masks[i] * (before[:, :B] + run), axis=0, keepdims=True))
        run = run + before[:, B:]
    rank = jnp.concatenate(ranks, axis=0)
    slot = jnp.where(remote, owner * CAP + rank.astype(jnp.int32), -1)
    slot_ref[...] = slot
    places = lax.broadcasted_iota(jnp.int32, (B, B), 0).astype(F32)
    what, where = [], []
    for i in range(F * H):
        what.append(
            jnp.concatenate([masks[i] * high[i : i + 1], masks[i] * low[i : i + 1]], axis=0)
        )
        where.append(jnp.where(places == rank[i : i + 1], 1.0, 0.0))
    what = jnp.concatenate(what, axis=1).astype(BF)
    where = jnp.concatenate(where, axis=1).astype(BF)
    req_ref[...] = lax.dot_general(what, where, NT, preferred_element_type=F32)
    grad = stack_tables(grad_ref[...])
    for base in range(0, OWNERS * CAP, BLOCK):
        block = jnp.dot(counts(slot, base), grad, preferred_element_type=F32)
        first = base // CAP
        last = (base + BLOCK) // CAP
        out_ref[first:last] = block.astype(BF).reshape(BLOCK // CAP, CAP, E)


def message_kernel(slots_ref, req_ref, got_ref, msg_ref):
    part = jnp.sum(got_ref[...].astype(F32), axis=0)
    for t in range(OWNERS):
        row = (t % 4 * 2 + t // 4 % 2) * PIECE
        high = req_ref[t : t + 1, :]
        low = req_ref[OWNERS + t : OWNERS + t + 1, :]
        tail = jnp.concatenate([part[row : row + PIECE], high, low], axis=0).astype(BF)
        msg_ref[t] = jnp.concatenate([slots_ref[t], tail], axis=0)


def hits_of(wanted, base):
    return jnp.concatenate([onehot(wanted[g : g + 1], base) for g in range(8)], axis=1)


def owner_kernel(got_ref, part_ref, wanted_ref, freq_ref):
    tails = [got_ref[t].astype(F32)[CAP:] for t in range(OWNERS)]
    pieces = [sum(t[:PIECE] for t in tails[y::4]) for y in range(4)]
    freq_ref[...] = jnp.concatenate(pieces, axis=0).astype(BF)
    high = jnp.concatenate([t[PIECE : PIECE + 1] for t in tails], axis=0)
    low = jnp.concatenate([t[PIECE + 1 :] for t in tails], axis=0)
    source = lax.broadcasted_iota(jnp.int32, (OWNERS, E), 0) % 4

    def placed(x):
        y = x
        for k in range(1, 4):
            y = jnp.where(source == k, pltpu.roll(x, CAP * k, 1), y)
        return y

    group = lax.broadcasted_iota(jnp.int32, (8, OWNERS), 0)
    member = lax.broadcasted_iota(jnp.int32, (8, OWNERS), 1) // 4
    fold = jnp.where(group == member, 1.0, 0.0).astype(BF)
    high = jnp.dot(fold, placed(high).astype(BF), preferred_element_type=F32)
    low = jnp.dot(fold, placed(low).astype(BF), preferred_element_type=F32)
    wanted = (high * 32.0 + low).astype(jnp.int32) - 1
    wanted_ref[...] = wanted
    grads = jnp.concatenate([got_ref[t][:CAP] for t in range(OWNERS)], axis=0)
    for base in range(0, RO, BLOCK):
        part = jnp.dot(hits_of(wanted, base), grads, preferred_element_type=F32)
        part_ref[base : base + BLOCK, :] = part.astype(BF)


def serve_kernel(wanted_ref, rows_ref, after_ref, out_ref):
    del after_ref
    wanted = wanted_ref[...]
    served = jnp.zeros((OWNERS * CAP, E), F32)
    for base in range(0, RO, BLOCK):
        rows = rows_ref[base : base + BLOCK, :].astype(BF)
        served = served + lax.dot_general(
            hits_of(wanted, base), rows, TN, preferred_element_type=F32
        )
    out_ref[...] = served.astype(BF).reshape(OWNERS, CAP, E)


def slice_kernel(got_ref, freq_ref, out_ref):
    out_ref[: RO // 8, :] = jnp.sum(got_ref[...].astype(F32), axis=0).astype(BF)
    out_ref[RO // 8 :, :] = freq_ref[...]


def pair_kernel(a_ref, b_ref, out_ref):
    out_ref[...] = (a_ref[...].astype(F32) + b_ref[...].astype(F32)).astype(BF)


def total_kernel(mine_ref, got_ref, after_ref, owned_ref, freq_ref):
    del after_ref
    total = (mine_ref[...].astype(F32) + got_ref[...].astype(F32)).astype(BF)
    owned_ref[...] = total[: RO // 8]
    for i in range(8):
        freq_ref[i] = total[RO // 8 :]


def spread_kernel(got_ref, owned_ref, out_ref):
    got = [got_ref[k].astype(F32) for k in range(8)]
    freq = [
        got[p * 4 + q][y * PIECE : (y + 1) * PIECE]
        for y in range(4)
        for q in range(4)
        for p in range(2)
    ]
    rows = jnp.concatenate([jnp.concatenate(freq, axis=0).astype(BF), owned_ref[...]], axis=0)
    for i in range(4):
        out_ref[i] = rows


def pool_frequent_kernel(index_ref, rows_ref, out_ref):
    index = index_ref[...]
    total = jnp.zeros((F * B, E), F32)
    for base in range(0, NF, BLOCK):
        rows = rows_ref[base : base + BLOCK, :].astype(BF)
        total = total + lax.dot_general(
            counts(index, base), rows, TN, preferred_element_type=F32
        )
    out_ref[...] = total


def pool_kernel(slot_ref, rows_ref, part_ref, out_ref):
    slot = slot_ref[...]
    total = part_ref[...]
    for base in range(0, OWNERS * CAP, BLOCK):
        rows = rows_ref[base : base + BLOCK, :]
        total = total + lax.dot_general(
            counts(slot, base), rows, TN, preferred_element_type=F32
        )
    for f in range(F):
        out_ref[:, f * E : (f + 1) * E] = total[f * B : (f + 1) * B].astype(BF)


def adagrad(rows, history, grad):
    grad = grad.astype(F32)
    new = history + grad * grad
    return rows - 0.5 * grad / jnp.sqrt(new + 1e-08), new


def adagrad_kernel(core_ref, mine_ref, other_ref, rows_ref, history_ref, updated_ref, new_ref):
    core = core_ref[0]
    part = updated_ref.shape[0] // 8
    first = mine_ref.shape[1] - part if part == RO // 8 else 0
    for got_ref, c in ((mine_ref, core), (other_ref, 1 - core)):
        for i in range(4):
            at = pl.ds(pl.multiple_of((2 * i + c) * part, part), part)
            updated_ref[at, :], new_ref[at, :] = adagrad(
                rows_ref[at, :], history_ref[at, :], got_ref[i, first : first + part, :]
            )


def swap(x, axes):
    return lax.all_to_all(x, axes, split_axis=0, concat_axis=0, tiled=True)


def window(z_hi, core, z_lo):
    return (z_hi - (core == 1 and z_lo < 4)) % 4


def z_hi_of(w, core, z_lo):
    return [z for z in range(4) if window(z, core, z_lo) == w][0]


def owner_groups():
    return [
        [
            ((z_hi_of(w, core, z) * 2 + core) * 8 + z) * 4 + y
            for z in range(8)
            for y in range(4)
        ]
        for core in range(2)
        for w in range(4)
    ]


def far_pairs(step):
    pairs = []
    for core in range(2):
        for w in range(4):
            other = w ^ 1 if step == 0 else (3 - w) % 4
            for z in range(8):
                a, b = z_hi_of(w, core, z), z_hi_of(other, core, z)
                pairs.append(((a * 2 + core) * 8 + z, (b * 2 + core) * 8 + z))
    return pairs


def far(x, step):
    return lax.ppermute(x, ("z_hi", "core", "z_pair", "z_odd"), far_pairs(step))


def to_owners(x):
    return lax.all_to_all(
        x,
        ("z_hi", "core", "z_pair", "z_odd", "y"),
        split_axis=0,
        concat_axis=0,
        tiled=True,
        axis_index_groups=owner_groups(),
    )


def body(index, frequent_rows, frequent_history, owned_rows, owned_history, grad):
    index = index.T
    near, plane = ("x", "core"), ("x", "core", "y")
    flat = F * B
    part = frequent_part(index, grad)
    part = swap(part.reshape(32, NF // 32, E), plane)
    slots, req, slot = call(
        slots_kernel,
        [
            sds((OWNERS, CAP, E), BF),
            sds((2 * OWNERS, E), F32),
            sds((F * H, B), jnp.int32),
        ],
        index,
        grad,
        flops=2 * RO * flat * E,
    )
    msg = call(message_kernel, [sds((OWNERS, MSG, E), BF)], slots, req, part)[0]
    got = to_owners(msg)
    owned, wanted, freq = call(
        owner_kernel,
        [sds((RO, E), BF), sds((8, E), jnp.int32), sds((NF // 64, E), BF)],
        got,
        flops=2 * RO * RO * E,
    )
    owned = swap(owned.reshape(8, RO // 8, E), near)
    both = call(slice_kernel, [sds((RO // 8 + NF // 64, E), BF)], owned, freq)[0]
    served = call(
        serve_kernel,
        [sds((OWNERS, CAP, E), BF)],
        wanted,
        owned_rows,
        both,
        flops=2 * RO * RO * E,
    )[0]
    returned = to_owners(served)
    got = far(both, 0)
    both = call(pair_kernel, [sds(both.shape, BF)], both, got, flops=PAIR_COST)[0]
    got = far(both, 1)
    got, returned = lax.optimization_barrier((got, returned))
    pooled = call(
        pool_frequent_kernel, [sds((flat, E), F32)], index, frequent_rows, flops=2 * NF * flat * E
    )[0]
    owned, freq = call(
        total_kernel, [sds((RO // 8, E), BF), sds((8, NF // 64, E), BF)], both, got, pooled
    )
    freq = swap(freq, ("z_odd", "y"))
    both = call(spread_kernel, [sds((4, (NF + RO) // 8, E), BF)], freq, owned)[0]
    mine = swap(both, "x")
    other = lax.ppermute(mine, "core", [(0, 1), (1, 0)])
    pooled = call(
        pool_kernel,
        [sds((B, F * E), BF)],
        slot,
        returned.reshape(OWNERS * CAP, E),
        pooled,
        flops=2 * RO * flat * E,
    )[0]
    core = lax.axis_index("core").reshape(1)
    updated_frequent, history_frequent = call(
        adagrad_kernel, [sds((NF, E), F32)] * 2, core, mine, other, frequent_rows, frequent_history
    )
    updated_owned, history_owned = call(
        adagrad_kernel, [sds((RO, E), F32)] * 2, core, mine, other, owned_rows, owned_history
    )
    return (pooled, updated_frequent, updated_owned, history_frequent, history_owned)


def solution(mesh):
    names = ("x", "z_hi", "core", "z_pair", "z_odd", "y")
    fine = Mesh(mesh.devices.reshape(4, 4, 2, 4, 2, 4), names)
    samples, table = names, names[3:]
    in_specs = (P(samples, None), P(), P(), P(table, None), P(table, None), P(samples, None))
    out_specs = (P(samples, None), P(), P(table, None), P(), P(table, None))
    return jax.shard_map(body, mesh=fine, in_specs=in_specs, out_specs=out_specs, check_vma=False)
```

```python
import functools
import jax
import jax.numpy as jnp
from jax import lax
from jax.experimental import pallas as pl
from jax.experimental.pallas import tpu as pltpu
from jax.sharding import Mesh, PartitionSpec as P

E = 128
F = 8
H = 4
B = 128
NF = 2048
RO = 1024
CAP = 32
OWNERS = 32
BLOCK = 256
PIECE = NF // 256
MSG = CAP + PIECE + 2
PAIR_COST = 10**12
BF = jnp.bfloat16
F32 = jnp.float32
NT = (((1,), (1,)), ((), ()))
TN = (((0,), (0,)), ((), ()))


def call(kernel, outs, *args, flops=0, vmem=40):
    moved = sum(a.size * a.dtype.itemsize for a in args)
    moved += sum(o.size * o.dtype.itemsize for o in outs)
    return pl.pallas_call(
        kernel,
        out_shape=outs,
        in_specs=[
            pl.BlockSpec(memory_space=pltpu.SMEM if len(a.shape) == 1 else pltpu.VMEM)
            for a in args
        ],
        out_specs=[pl.BlockSpec(memory_space=pltpu.VMEM)] * len(outs),
        compiler_params=pltpu.CompilerParams(vmem_limit_bytes=vmem * 1024 * 1024),
        cost_estimate=pl.CostEstimate(flops=flops, bytes_accessed=moved, transcendentals=0),
    )(*args)


def sds(shape, dtype):
    return jax.ShapeDtypeStruct(shape, dtype)


def onehot(positions, base):
    near = (positions - base).astype(F32).astype(BF)
    rows = lax.broadcasted_iota(jnp.int32, (BLOCK, positions.shape[1]), 0).astype(F32).astype(BF)
    total = None
    for i in range(positions.shape[0]):
        hit = jnp.where(rows == near[i : i + 1], jnp.ones((), BF), jnp.zeros((), BF))
        total = hit if total is None else total + hit
    return total


def counts(positions, base):
    return jnp.concatenate([onehot(positions[f * H : (f + 1) * H], base) for f in range(F)], axis=1)


def stack_tables(grad):
    return jnp.concatenate([grad[:, f * E : (f + 1) * E] for f in range(F)], axis=0)


def frequent_kernel(index_hbm, grad_hbm, part_ref, index_ref, grad_ref, sems):
    index_copy = pltpu.make_async_copy(index_hbm, index_ref, sems.at[0])
    grad_copy = pltpu.make_async_copy(grad_hbm, grad_ref, sems.at[1])
    index_copy.start()
    grad_copy.start()
    index_copy.wait()
    index = index_ref[...]
    first = counts(index, 0)
    grad_copy.wait()
    grad = stack_tables(grad_ref[...])
    for base in range(0, NF, BLOCK):
        hits = counts(index, base) if base else first
        part = jnp.dot(hits, grad, preferred_element_type=F32)
        part_ref[base : base + BLOCK, :] = part.astype(BF)


def frequent_part(index, grad):
    return pl.pallas_call(
        frequent_kernel,
        out_shape=sds((NF, E), BF),
        in_specs=[pl.BlockSpec(memory_space=pl.ANY)] * 2,
        out_specs=pl.BlockSpec(memory_space=pltpu.VMEM),
        scratch_shapes=[
            pltpu.VMEM(index.shape, index.dtype),
            pltpu.VMEM(grad.shape, grad.dtype),
            pltpu.SemaphoreType.DMA((2,)),
        ],
        compiler_params=pltpu.CompilerParams(vmem_limit_bytes=60 * 1024 * 1024),
    )(index, grad)


def slots_kernel(index_ref, grad_ref, out_ref, req_ref, slot_ref):
    index = index_ref[...]
    remote = index >= NF
    offset = index - NF
    owner = jnp.where(remote, offset // RO, -1)
    wanted = offset % RO + 1
    high = (wanted // 32).astype(F32)
    low = (wanted % 32).astype(F32)
    owners = lax.broadcasted_iota(jnp.int32, (OWNERS, B), 0)
    masks = [
        jnp.where(owners == owner[i : i + 1], 1.0, 0.0).astype(F32) for i in range(F * H)
    ]
    mask = jnp.concatenate(masks, axis=0).astype(BF)
    row = lax.broadcasted_iota(jnp.int32, (B, 2 * B), 0)
    col = lax.broadcasted_iota(jnp.int32, (B, 2 * B), 1)
    ones = jnp.where((col >= B) | (row < col), 1.0, 0.0).astype(BF)
    earlier = jnp.dot(mask, ones, preferred_element_type=F32)
    run = jnp.zeros((OWNERS, B), F32)
    ranks = []
    for i in range(F * H):
        before = earlier[i * OWNERS : (i + 1) * OWNERS]
        ranks.append(jnp.sum(masks[i] * (before[:, :B] + run), axis=0, keepdims=True))
        run = run + before[:, B:]
    rank = jnp.concatenate(ranks, axis=0)
    slot = jnp.where(remote, owner * CAP + rank.astype(jnp.int32), -1)
    slot_ref[...] = slot
    places = lax.broadcasted_iota(jnp.int32, (B, B), 0).astype(F32)
    what, where = [], []
    for i in range(F * H):
        what.append(
            jnp.concatenate([masks[i] * high[i : i + 1], masks[i] * low[i : i + 1]], axis=0)
        )
        where.append(jnp.where(places == rank[i : i + 1], 1.0, 0.0))
    what = jnp.concatenate(what, axis=1).astype(BF)
    where = jnp.concatenate(where, axis=1).astype(BF)
    req_ref[...] = lax.dot_general(what, where, NT, preferred_element_type=F32)
    grad = stack_tables(grad_ref[...])
    for base in range(0, OWNERS * CAP, BLOCK):
        block = jnp.dot(counts(slot, base), grad, preferred_element_type=F32)
        first = base // CAP
        last = (base + BLOCK) // CAP
        out_ref[first:last] = block.astype(BF).reshape(BLOCK // CAP, CAP, E)


def message_kernel(slots_ref, req_ref, got_ref, msg_ref):
    part = jnp.sum(got_ref[...].astype(F32), axis=0)
    for t in range(OWNERS):
        row = (t % 4 * 2 + t // 4 % 2) * PIECE
        high = req_ref[t : t + 1, :]
        low = req_ref[OWNERS + t : OWNERS + t + 1, :]
        tail = jnp.concatenate([part[row : row + PIECE], high, low], axis=0).astype(BF)
        msg_ref[t] = jnp.concatenate([slots_ref[t], tail], axis=0)


def hits_of(wanted, base):
    return jnp.concatenate([onehot(wanted[g : g + 1], base) for g in range(8)], axis=1)


def owner_kernel(got_ref, part_ref, wanted_ref, freq_ref):
    tails = [got_ref[t].astype(F32)[CAP:] for t in range(OWNERS)]
    pieces = [sum(t[:PIECE] for t in tails[y::4]) for y in range(4)]
    freq_ref[...] = jnp.concatenate(pieces, axis=0).astype(BF)
    high = jnp.concatenate([t[PIECE : PIECE + 1] for t in tails], axis=0)
    low = jnp.concatenate([t[PIECE + 1 :] for t in tails], axis=0)
    source = lax.broadcasted_iota(jnp.int32, (OWNERS, E), 0) % 4

    def placed(x):
        y = x
        for k in range(1, 4):
            y = jnp.where(source == k, pltpu.roll(x, CAP * k, 1), y)
        return y

    group = lax.broadcasted_iota(jnp.int32, (8, OWNERS), 0)
    member = lax.broadcasted_iota(jnp.int32, (8, OWNERS), 1) // 4
    fold = jnp.where(group == member, 1.0, 0.0).astype(BF)
    high = jnp.dot(fold, placed(high).astype(BF), preferred_element_type=F32)
    low = jnp.dot(fold, placed(low).astype(BF), preferred_element_type=F32)
    wanted = (high * 32.0 + low).astype(jnp.int32) - 1
    wanted_ref[...] = wanted
    grads = jnp.concatenate([got_ref[t][:CAP] for t in range(OWNERS)], axis=0)
    for base in range(0, RO, BLOCK):
        part = jnp.dot(hits_of(wanted, base), grads, preferred_element_type=F32)
        part_ref[base : base + BLOCK, :] = part.astype(BF)


def serve_kernel(wanted_ref, rows_ref, out_ref):
    wanted = wanted_ref[...]
    served = jnp.zeros((OWNERS * CAP, E), F32)
    for base in range(0, RO, BLOCK):
        rows = rows_ref[base : base + BLOCK, :].astype(BF)
        served = served + lax.dot_general(
            hits_of(wanted, base), rows, TN, preferred_element_type=F32
        )
    out_ref[...] = served.astype(BF).reshape(OWNERS, CAP, E)


def slice_kernel(got_ref, freq_ref, out_ref):
    out_ref[: RO // 8, :] = jnp.sum(got_ref[...].astype(F32), axis=0).astype(BF)
    out_ref[RO // 8 :, :] = freq_ref[...]


def pair_kernel(a_ref, b_ref, out_ref):
    out_ref[...] = (a_ref[...].astype(F32) + b_ref[...].astype(F32)).astype(BF)


def total_kernel(mine_ref, got_ref, after_ref, owned_ref, freq_ref):
    del after_ref
    total = (mine_ref[...].astype(F32) + got_ref[...].astype(F32)).astype(BF)
    owned_ref[...] = total[: RO // 8]
    for i in range(8):
        freq_ref[i] = total[RO // 8 :]


def spread_kernel(got_ref, owned_ref, out_ref):
    got = [got_ref[k].astype(F32) for k in range(8)]
    freq = [
        got[p * 4 + q][y * PIECE : (y + 1) * PIECE]
        for y in range(4)
        for q in range(4)
        for p in range(2)
    ]
    rows = jnp.concatenate([jnp.concatenate(freq, axis=0).astype(BF), owned_ref[...]], axis=0)
    for i in range(4):
        out_ref[i] = rows


def pool_frequent_kernel(index_ref, rows_ref, out_ref):
    index = index_ref[...]
    total = jnp.zeros((F * B, E), F32)
    for base in range(0, NF, BLOCK):
        rows = rows_ref[base : base + BLOCK, :].astype(BF)
        total = total + lax.dot_general(
            counts(index, base), rows, TN, preferred_element_type=F32
        )
    out_ref[...] = total


def pool_kernel(slot_ref, rows_ref, part_ref, out_ref):
    slot = slot_ref[...]
    total = part_ref[...]
    for base in range(0, OWNERS * CAP, BLOCK):
        rows = rows_ref[base : base + BLOCK, :]
        total = total + lax.dot_general(
            counts(slot, base), rows, TN, preferred_element_type=F32
        )
    for f in range(F):
        out_ref[:, f * E : (f + 1) * E] = total[f * B : (f + 1) * B].astype(BF)


def adagrad(rows, history, grad):
    grad = grad.astype(F32)
    new = history + grad * grad
    return rows - 0.5 * grad / jnp.sqrt(new + 1e-08), new


def adagrad_kernel(core_ref, mine_ref, other_ref, rows_ref, history_ref, updated_ref, new_ref):
    core = core_ref[0]
    part = updated_ref.shape[0] // 8
    first = mine_ref.shape[1] - part if part == RO // 8 else 0
    for got_ref, c in ((mine_ref, core), (other_ref, 1 - core)):
        for i in range(4):
            at = pl.ds(pl.multiple_of((2 * i + c) * part, part), part)
            updated_ref[at, :], new_ref[at, :] = adagrad(
                rows_ref[at, :], history_ref[at, :], got_ref[i, first : first + part, :]
            )


def swap(x, axes):
    return lax.all_to_all(x, axes, split_axis=0, concat_axis=0, tiled=True)


def window(z_hi, core, z_lo):
    return (z_hi - (core == 1 and z_lo < 4)) % 4


def z_hi_of(w, core, z_lo):
    return [z for z in range(4) if window(z, core, z_lo) == w][0]


def owner_groups():
    return [
        [
            ((z_hi_of(w, core, z) * 2 + core) * 8 + z) * 4 + y
            for z in range(8)
            for y in range(4)
        ]
        for core in range(2)
        for w in range(4)
    ]


def far_pairs(step):
    pairs = []
    for core in range(2):
        for w in range(4):
            other = w ^ 1 if step == 0 else (3 - w) % 4
            for z in range(8):
                a, b = z_hi_of(w, core, z), z_hi_of(other, core, z)
                pairs.append(((a * 2 + core) * 8 + z, (b * 2 + core) * 8 + z))
    return pairs


def far(x, step):
    return lax.ppermute(x, ("z_hi", "core", "z_pair", "z_odd"), far_pairs(step))


def to_owners(x):
    return lax.all_to_all(
        x,
        ("z_hi", "core", "z_pair", "z_odd", "y"),
        split_axis=0,
        concat_axis=0,
        tiled=True,
        axis_index_groups=owner_groups(),
    )


def body(index, frequent_rows, frequent_history, owned_rows, owned_history, grad):
    index = index.T
    near, plane = ("x", "core"), ("x", "core", "y")
    flat = F * B
    part = frequent_part(index, grad)
    part = swap(part.reshape(32, NF // 32, E), plane)
    slots, req, slot = call(
        slots_kernel,
        [
            sds((OWNERS, CAP, E), BF),
            sds((2 * OWNERS, E), F32),
            sds((F * H, B), jnp.int32),
        ],
        index,
        grad,
        flops=2 * RO * flat * E,
    )
    msg = call(message_kernel, [sds((OWNERS, MSG, E), BF)], slots, req, part)[0]
    got = to_owners(msg)
    owned, wanted, freq = call(
        owner_kernel,
        [sds((RO, E), BF), sds((8, E), jnp.int32), sds((NF // 64, E), BF)],
        got,
        flops=2 * RO * RO * E,
    )
    owned = swap(owned.reshape(8, RO // 8, E), near)
    both = call(slice_kernel, [sds((RO // 8 + NF // 64, E), BF)], owned, freq)[0]
    served = call(
        serve_kernel,
        [sds((OWNERS, CAP, E), BF)],
        wanted,
        owned_rows,
        flops=2 * RO * RO * E,
    )[0]
    served, both = lax.optimization_barrier((served, both))
    returned = to_owners(served)
    got = far(both, 0)
    both = call(pair_kernel, [sds(both.shape, BF)], both, got, flops=PAIR_COST)[0]
    got = far(both, 1)
    got, returned = lax.optimization_barrier((got, returned))
    pooled = call(
        pool_frequent_kernel, [sds((flat, E), F32)], index, frequent_rows, flops=2 * NF * flat * E
    )[0]
    owned, freq = call(
        total_kernel, [sds((RO // 8, E), BF), sds((8, NF // 64, E), BF)], both, got, pooled
    )
    freq = swap(freq, ("z_odd", "y"))
    both = call(spread_kernel, [sds((4, (NF + RO) // 8, E), BF)], freq, owned)[0]
    mine = swap(both, "x")
    other = lax.ppermute(mine, "core", [(0, 1), (1, 0)])
    pooled = call(
        pool_kernel,
        [sds((B, F * E), BF)],
        slot,
        returned.reshape(OWNERS * CAP, E),
        pooled,
        flops=2 * RO * flat * E,
    )[0]
    core = lax.axis_index("core").reshape(1)
    updated_frequent, history_frequent = call(
        adagrad_kernel, [sds((NF, E), F32)] * 2, core, mine, other, frequent_rows, frequent_history
    )
    updated_owned, history_owned = call(
        adagrad_kernel, [sds((RO, E), F32)] * 2, core, mine, other, owned_rows, owned_history
    )
    return (pooled, updated_frequent, updated_owned, history_frequent, history_owned)


def solution(mesh):
    names = ("x", "z_hi", "core", "z_pair", "z_odd", "y")
    fine = Mesh(mesh.devices.reshape(4, 4, 2, 4, 2, 4), names)
    samples, table = names, names[3:]
    in_specs = (P(samples, None), P(), P(), P(table, None), P(table, None), P(samples, None))
    out_specs = (P(samples, None), P(), P(table, None), P(), P(table, None))
    return jax.shard_map(body, mesh=fine, in_specs=in_specs, out_specs=out_specs, check_vma=False)
```

```python
import functools
import jax
import jax.numpy as jnp
from jax import lax
from jax.experimental import pallas as pl
from jax.experimental.pallas import tpu as pltpu
from jax.sharding import Mesh, PartitionSpec as P

E = 128
F = 8
H = 4
B = 128
NF = 2048
RO = 1024
CAP = 32
OWNERS = 32
BLOCK = 256
PIECE = NF // 256
MSG = CAP + PIECE + 2
PAIR_COST = 10**12
BF = jnp.bfloat16
F32 = jnp.float32
NT = (((1,), (1,)), ((), ()))
TN = (((0,), (0,)), ((), ()))


def call(kernel, outs, *args, flops=0, vmem=40):
    moved = sum(a.size * a.dtype.itemsize for a in args)
    moved += sum(o.size * o.dtype.itemsize for o in outs)
    return pl.pallas_call(
        kernel,
        out_shape=outs,
        in_specs=[
            pl.BlockSpec(memory_space=pltpu.SMEM if len(a.shape) == 1 else pltpu.VMEM)
            for a in args
        ],
        out_specs=[pl.BlockSpec(memory_space=pltpu.VMEM)] * len(outs),
        compiler_params=pltpu.CompilerParams(vmem_limit_bytes=vmem * 1024 * 1024),
        cost_estimate=pl.CostEstimate(flops=flops, bytes_accessed=moved, transcendentals=0),
    )(*args)


def sds(shape, dtype):
    return jax.ShapeDtypeStruct(shape, dtype)


def onehot(positions, base):
    near = (positions - base).astype(F32).astype(BF)
    rows = lax.broadcasted_iota(jnp.int32, (BLOCK, positions.shape[1]), 0).astype(F32).astype(BF)
    total = None
    for i in range(positions.shape[0]):
        hit = jnp.where(rows == near[i : i + 1], jnp.ones((), BF), jnp.zeros((), BF))
        total = hit if total is None else total + hit
    return total


def counts(positions, base):
    return jnp.concatenate([onehot(positions[f * H : (f + 1) * H], base) for f in range(F)], axis=1)


def stack_tables(grad):
    return jnp.concatenate([grad[:, f * E : (f + 1) * E] for f in range(F)], axis=0)


def frequent_kernel(index_hbm, grad_hbm, part_ref, index_ref, grad_ref, hits_ref, sems):
    index_copy = pltpu.make_async_copy(index_hbm, index_ref, sems.at[0])
    grad_copy = pltpu.make_async_copy(grad_hbm, grad_ref, sems.at[1])
    index_copy.start()
    grad_copy.start()
    index_copy.wait()
    index = index_ref[...]
    early = hits_ref.shape[0]
    for base in range(0, early, BLOCK):
        hits_ref[base : base + BLOCK, :] = counts(index, base)
    grad_copy.wait()
    grad = stack_tables(grad_ref[...])
    for base in range(0, NF, BLOCK):
        hits = hits_ref[base : base + BLOCK, :] if base < early else counts(index, base)
        part = jnp.dot(hits, grad, preferred_element_type=F32)
        part_ref[base : base + BLOCK, :] = part.astype(BF)


def frequent_part(index, grad):
    return pl.pallas_call(
        frequent_kernel,
        out_shape=sds((NF, E), BF),
        in_specs=[pl.BlockSpec(memory_space=pl.ANY)] * 2,
        out_specs=pl.BlockSpec(memory_space=pltpu.VMEM),
        scratch_shapes=[
            pltpu.VMEM(index.shape, index.dtype),
            pltpu.VMEM(grad.shape, grad.dtype),
            pltpu.VMEM((NF // 2, F * B), BF),
            pltpu.SemaphoreType.DMA((2,)),
        ],
        compiler_params=pltpu.CompilerParams(vmem_limit_bytes=60 * 1024 * 1024),
    )(index, grad)


def slots_kernel(index_ref, grad_ref, out_ref, req_ref, slot_ref):
    index = index_ref[...]
    remote = index >= NF
    offset = index - NF
    owner = jnp.where(remote, offset // RO, -1)
    wanted = offset % RO + 1
    high = (wanted // 32).astype(F32)
    low = (wanted % 32).astype(F32)
    owners = lax.broadcasted_iota(jnp.int32, (OWNERS, B), 0)
    masks = [
        jnp.where(owners == owner[i : i + 1], 1.0, 0.0).astype(F32) for i in range(F * H)
    ]
    mask = jnp.concatenate(masks, axis=0).astype(BF)
    row = lax.broadcasted_iota(jnp.int32, (B, 2 * B), 0)
    col = lax.broadcasted_iota(jnp.int32, (B, 2 * B), 1)
    ones = jnp.where((col >= B) | (row < col), 1.0, 0.0).astype(BF)
    earlier = jnp.dot(mask, ones, preferred_element_type=F32)
    run = jnp.zeros((OWNERS, B), F32)
    ranks = []
    for i in range(F * H):
        before = earlier[i * OWNERS : (i + 1) * OWNERS]
        ranks.append(jnp.sum(masks[i] * (before[:, :B] + run), axis=0, keepdims=True))
        run = run + before[:, B:]
    rank = jnp.concatenate(ranks, axis=0)
    slot = jnp.where(remote, owner * CAP + rank.astype(jnp.int32), -1)
    slot_ref[...] = slot
    places = lax.broadcasted_iota(jnp.int32, (B, B), 0).astype(F32)
    what, where = [], []
    for i in range(F * H):
        what.append(
            jnp.concatenate([masks[i] * high[i : i + 1], masks[i] * low[i : i + 1]], axis=0)
        )
        where.append(jnp.where(places == rank[i : i + 1], 1.0, 0.0))
    what = jnp.concatenate(what, axis=1).astype(BF)
    where = jnp.concatenate(where, axis=1).astype(BF)
    req_ref[...] = lax.dot_general(what, where, NT, preferred_element_type=F32)
    grad = stack_tables(grad_ref[...])
    for base in range(0, OWNERS * CAP, BLOCK):
        block = jnp.dot(counts(slot, base), grad, preferred_element_type=F32)
        first = base // CAP
        last = (base + BLOCK) // CAP
        out_ref[first:last] = block.astype(BF).reshape(BLOCK // CAP, CAP, E)


def message_kernel(slots_ref, req_ref, got_ref, msg_ref):
    part = jnp.sum(got_ref[...].astype(F32), axis=0)
    for t in range(OWNERS):
        row = (t % 4 * 2 + t // 4 % 2) * PIECE
        high = req_ref[t : t + 1, :]
        low = req_ref[OWNERS + t : OWNERS + t + 1, :]
        tail = jnp.concatenate([part[row : row + PIECE], high, low], axis=0).astype(BF)
        msg_ref[t] = jnp.concatenate([slots_ref[t], tail], axis=0)


def hits_of(wanted, base):
    return jnp.concatenate([onehot(wanted[g : g + 1], base) for g in range(8)], axis=1)


def owner_kernel(got_ref, part_ref, wanted_ref, freq_ref):
    tails = [got_ref[t].astype(F32)[CAP:] for t in range(OWNERS)]
    pieces = [sum(t[:PIECE] for t in tails[y::4]) for y in range(4)]
    freq_ref[...] = jnp.concatenate(pieces, axis=0).astype(BF)
    high = jnp.concatenate([t[PIECE : PIECE + 1] for t in tails], axis=0)
    low = jnp.concatenate([t[PIECE + 1 :] for t in tails], axis=0)
    source = lax.broadcasted_iota(jnp.int32, (OWNERS, E), 0) % 4

    def placed(x):
        y = x
        for k in range(1, 4):
            y = jnp.where(source == k, pltpu.roll(x, CAP * k, 1), y)
        return y

    group = lax.broadcasted_iota(jnp.int32, (8, OWNERS), 0)
    member = lax.broadcasted_iota(jnp.int32, (8, OWNERS), 1) // 4
    fold = jnp.where(group == member, 1.0, 0.0).astype(BF)
    high = jnp.dot(fold, placed(high).astype(BF), preferred_element_type=F32)
    low = jnp.dot(fold, placed(low).astype(BF), preferred_element_type=F32)
    wanted = (high * 32.0 + low).astype(jnp.int32) - 1
    wanted_ref[...] = wanted
    grads = jnp.concatenate([got_ref[t][:CAP] for t in range(OWNERS)], axis=0)
    for base in range(0, RO, BLOCK):
        part = jnp.dot(hits_of(wanted, base), grads, preferred_element_type=F32)
        part_ref[base : base + BLOCK, :] = part.astype(BF)


def serve_kernel(wanted_ref, rows_ref, out_ref):
    wanted = wanted_ref[...]
    served = jnp.zeros((OWNERS * CAP, E), F32)
    for base in range(0, RO, BLOCK):
        rows = rows_ref[base : base + BLOCK, :].astype(BF)
        served = served + lax.dot_general(
            hits_of(wanted, base), rows, TN, preferred_element_type=F32
        )
    out_ref[...] = served.astype(BF).reshape(OWNERS, CAP, E)


def slice_kernel(got_ref, freq_ref, out_ref):
    out_ref[: RO // 8, :] = jnp.sum(got_ref[...].astype(F32), axis=0).astype(BF)
    out_ref[RO // 8 :, :] = freq_ref[...]


def pair_kernel(a_ref, b_ref, out_ref):
    out_ref[...] = (a_ref[...].astype(F32) + b_ref[...].astype(F32)).astype(BF)


def total_kernel(mine_ref, got_ref, after_ref, owned_ref, freq_ref):
    del after_ref
    total = (mine_ref[...].astype(F32) + got_ref[...].astype(F32)).astype(BF)
    owned_ref[...] = total[: RO // 8]
    for i in range(8):
        freq_ref[i] = total[RO // 8 :]


def spread_kernel(got_ref, owned_ref, out_ref):
    got = [got_ref[k].astype(F32) for k in range(8)]
    freq = [
        got[p * 4 + q][y * PIECE : (y + 1) * PIECE]
        for y in range(4)
        for q in range(4)
        for p in range(2)
    ]
    rows = jnp.concatenate([jnp.concatenate(freq, axis=0).astype(BF), owned_ref[...]], axis=0)
    for i in range(4):
        out_ref[i] = rows


def pool_frequent_kernel(index_ref, rows_ref, out_ref):
    index = index_ref[...]
    total = jnp.zeros((F * B, E), F32)
    for base in range(0, NF, BLOCK):
        rows = rows_ref[base : base + BLOCK, :].astype(BF)
        total = total + lax.dot_general(
            counts(index, base), rows, TN, preferred_element_type=F32
        )
    out_ref[...] = total


def pool_kernel(slot_ref, rows_ref, part_ref, out_ref):
    slot = slot_ref[...]
    total = part_ref[...]
    for base in range(0, OWNERS * CAP, BLOCK):
        rows = rows_ref[base : base + BLOCK, :]
        total = total + lax.dot_general(
            counts(slot, base), rows, TN, preferred_element_type=F32
        )
    for f in range(F):
        out_ref[:, f * E : (f + 1) * E] = total[f * B : (f + 1) * B].astype(BF)


def adagrad(rows, history, grad):
    grad = grad.astype(F32)
    new = history + grad * grad
    return rows - 0.5 * grad * lax.rsqrt(new + 1e-08), new


def adagrad_kernel(core_ref, mine_ref, other_ref, rows_ref, history_ref, updated_ref, new_ref):
    core = core_ref[0]
    part = updated_ref.shape[0] // 8
    first = mine_ref.shape[1] - part if part == RO // 8 else 0
    for got_ref, c in ((mine_ref, core), (other_ref, 1 - core)):
        for i in range(4):
            at = pl.ds(pl.multiple_of((2 * i + c) * part, part), part)
            updated_ref[at, :], new_ref[at, :] = adagrad(
                rows_ref[at, :], history_ref[at, :], got_ref[i, first : first + part, :]
            )


def swap(x, axes):
    return lax.all_to_all(x, axes, split_axis=0, concat_axis=0, tiled=True)


def window(z_hi, core, z_lo):
    return (z_hi - (core == 1 and z_lo < 4)) % 4


def z_hi_of(w, core, z_lo):
    return [z for z in range(4) if window(z, core, z_lo) == w][0]


def owner_groups():
    return [
        [
            ((z_hi_of(w, core, z) * 2 + core) * 8 + z) * 4 + y
            for z in range(8)
            for y in range(4)
        ]
        for core in range(2)
        for w in range(4)
    ]


def far_pairs(step):
    pairs = []
    for core in range(2):
        for w in range(4):
            other = w ^ 1 if step == 0 else (3 - w) % 4
            for z in range(8):
                a, b = z_hi_of(w, core, z), z_hi_of(other, core, z)
                pairs.append(((a * 2 + core) * 8 + z, (b * 2 + core) * 8 + z))
    return pairs


def far(x, step):
    return lax.ppermute(x, ("z_hi", "core", "z_pair", "z_odd"), far_pairs(step))


def to_owners(x):
    return lax.all_to_all(
        x,
        ("z_hi", "core", "z_pair", "z_odd", "y"),
        split_axis=0,
        concat_axis=0,
        tiled=True,
        axis_index_groups=owner_groups(),
    )


def body(index, frequent_rows, frequent_history, owned_rows, owned_history, grad):
    index = index.T
    near, plane = ("x", "core"), ("x", "core", "y")
    flat = F * B
    part = frequent_part(index, grad)
    part = swap(part.reshape(32, NF // 32, E), plane)
    slots, req, slot = call(
        slots_kernel,
        [
            sds((OWNERS, CAP, E), BF),
            sds((2 * OWNERS, E), F32),
            sds((F * H, B), jnp.int32),
        ],
        index,
        grad,
        flops=2 * RO * flat * E,
    )
    msg = call(message_kernel, [sds((OWNERS, MSG, E), BF)], slots, req, part)[0]
    got = to_owners(msg)
    owned, wanted, freq = call(
        owner_kernel,
        [sds((RO, E), BF), sds((8, E), jnp.int32), sds((NF // 64, E), BF)],
        got,
        flops=2 * RO * RO * E,
    )
    owned = swap(owned.reshape(8, RO // 8, E), near)
    both = call(slice_kernel, [sds((RO // 8 + NF // 64, E), BF)], owned, freq)[0]
    served = call(
        serve_kernel,
        [sds((OWNERS, CAP, E), BF)],
        wanted,
        owned_rows,
        flops=2 * RO * RO * E,
    )[0]
    served, both = lax.optimization_barrier((served, both))
    returned = to_owners(served)
    got = far(both, 0)
    both = call(pair_kernel, [sds(both.shape, BF)], both, got, flops=PAIR_COST)[0]
    got = far(both, 1)
    got, returned = lax.optimization_barrier((got, returned))
    pooled = call(
        pool_frequent_kernel, [sds((flat, E), F32)], index, frequent_rows, flops=2 * NF * flat * E
    )[0]
    owned, freq = call(
        total_kernel, [sds((RO // 8, E), BF), sds((8, NF // 64, E), BF)], both, got, pooled
    )
    freq = swap(freq, ("z_odd", "y"))
    both = call(spread_kernel, [sds((4, (NF + RO) // 8, E), BF)], freq, owned)[0]
    mine = swap(both, "x")
    other = lax.ppermute(mine, "core", [(0, 1), (1, 0)])
    pooled = call(
        pool_kernel,
        [sds((B, F * E), BF)],
        slot,
        returned.reshape(OWNERS * CAP, E),
        pooled,
        flops=2 * RO * flat * E,
    )[0]
    core = lax.axis_index("core").reshape(1)
    updated_frequent, history_frequent = call(
        adagrad_kernel, [sds((NF, E), F32)] * 2, core, mine, other, frequent_rows, frequent_history
    )
    updated_owned, history_owned = call(
        adagrad_kernel, [sds((RO, E), F32)] * 2, core, mine, other, owned_rows, owned_history
    )
    return (pooled, updated_frequent, updated_owned, history_frequent, history_owned)


def solution(mesh):
    names = ("x", "z_hi", "core", "z_pair", "z_odd", "y")
    fine = Mesh(mesh.devices.reshape(4, 4, 2, 4, 2, 4), names)
    samples, table = names, names[3:]
    in_specs = (P(samples, None), P(), P(), P(table, None), P(table, None), P(samples, None))
    out_specs = (P(samples, None), P(), P(table, None), P(), P(table, None))
    return jax.shard_map(body, mesh=fine, in_specs=in_specs, out_specs=out_specs, check_vma=False)
```
